32 devices in a mesh: gx: 4 (over z), gy: 4 (over x, core), gz: 2 (over y).
Axes of the slice: x: 2, y: 2, z: 4, core: 2. Of those that a mesh axis runs over, the one named last changes fastest.
Arguments:
- gas: float32 [6, 32, 32, 256], P(None, 'gx', 'gy', 'gz'), may hold values from -1.5 to 6, as said below
- parcels: float32 [2048, 5, 128], P(('gx', 'gy', 'gz')), may hold values from -1 to 2, as said below
- home_cell_index: int32 [2048, 128], P(('gx', 'gy', 'gz')), may hold values from 0 to 8191
- order: int32 [32, 64], P(('gx', 'gy', 'gz')), may hold values from 0 to 63, each once within a row
- counts: int32 [32, 3], P(('gx', 'gy', 'gz')), may hold values from 0 to 32, as said below
Outputs:
- gas_out: float32 [6, 32, 32, 256], P(None, 'gx', 'gy', 'gz')
- moved_parcels: float32 [2048, 5, 128], P(('gx', 'gy', 'gz'))
The draws below stay inside these ranges and needn't reach their ends.
Inputs may be any that keep to these rules, and one draw needn't show every extreme that they name: `gas`: gas density lies in 0.8 to 1.6, pressure in 0.8 to 1.6, velocities within 0.8, vapour fraction in 0.05 to 0.3. `parcels`: parcel masses lie in 0.2 to 2, temperatures in 0.3 to 1.2, velocities in -1 to 1.5. `counts`: kept is at most 32, forward and back each at most 16; each bound is reached in every draw.
All inputs are finite; a program needn't handle non-finite values.
Results may differ from the reference program's by a relative error of at most 0.00002.
Values sent between devices are 32-bit elements; how exact they have to be, the bound alone decides.
A program may use at most 64 MiB of HBM per device.

```python
import jax
import jax.numpy as jnp
from jax import lax

AXIAL_CELLS = 8
CROSSWISE_CELLS = 8
LATERAL_CELLS = 128
BLK_DEV = 64
NX = 32
NY = 32
NZ = 256
PACKET_ROOM = 2048
N_GX = 4
N_GY = 4
N_GZ = 2
DEVICES = 32


GAMMA = 1.4


def draw_gas(key, part):
    chance_generator_inputs = jax.random.split(jax.random.fold_in(key, 5), 5)
    grid_shape = (NX, NY, NZ)
    density = jax.random.uniform(chance_generator_inputs[0], grid_shape, jnp.float32, 0.8, 1.6)
    spray_drop_momentum_tendency = jax.random.uniform(chance_generator_inputs[1], (3,) + grid_shape, jnp.float32, -0.5, 0.5)
    pressure = jax.random.uniform(chance_generator_inputs[2], grid_shape, jnp.float32, 0.8, 1.6)
    fraction = jax.random.uniform(chance_generator_inputs[3], grid_shape, jnp.float32, 0.05, 0.3)
    momentum = density[None] * spray_drop_momentum_tendency
    energy = pressure / (GAMMA - 1.0) + 0.5 * density * jnp.sum(spray_drop_momentum_tendency * spray_drop_momentum_tendency, axis=0)
    return jnp.concatenate([density[None], momentum, energy[None], (density * fraction)[None]], axis=0).astype(jnp.float32)


def draw_parcels(key, part):
    chance_generator_inputs = jax.random.split(jax.random.fold_in(key, 7), 3)
    spray_drop_momentum_tendency = jax.random.uniform(chance_generator_inputs[0], (PACKET_ROOM, 3, 128), jnp.float32, -1.0, 1.0)
    spray_drop_ln_multiplicity = jax.random.uniform(chance_generator_inputs[1], (PACKET_ROOM, 1, 128), jnp.float32, jnp.log(0.2), jnp.log(2.0))
    spray_drop_warmth_measure = jax.random.uniform(chance_generator_inputs[2], (PACKET_ROOM, 1, 128), jnp.float32, 0.3, 1.2)
    return jnp.concatenate([spray_drop_momentum_tendency, jnp.exp(spray_drop_ln_multiplicity), spray_drop_warmth_measure], axis=1).astype(jnp.float32)


def draw_counts(key, part):
    chance_generator_inputs = jax.random.split(jax.random.fold_in(key, 17), 3)
    dev_ids = jnp.arange(DEVICES, dtype=jnp.int32)
    slab_dev = dev_ids // (N_GY * N_GZ)
    half_cap = BLK_DEV // 2
    move_cap = BLK_DEV // 4
    limit = half_cap * (slab_dev + 1) // N_GX
    kept = jax.random.randint(chance_generator_inputs[0], (DEVICES,), 0, limit + 1)
    kept = jnp.where(slab_dev == N_GX - 1, half_cap, kept)
    forward = jax.random.randint(chance_generator_inputs[1], (DEVICES,), 0, move_cap + 1)
    forward = jnp.where(dev_ids == 0, move_cap, forward)
    backward = jax.random.randint(chance_generator_inputs[2], (DEVICES,), 0, move_cap + 1)
    backward = jnp.where(dev_ids == N_GY * N_GZ, move_cap, backward)
    return jnp.stack([kept, forward, backward], axis=1).astype(jnp.int32)


def set_ends(array, key, least, top_value):
    longest = array.shape.index(max(array.shape))
    spots = []
    for shift in (0, 1):
        where = [jax.random.randint(jax.random.fold_in(key, axis), (), 0, length) for axis, length in enumerate(array.shape)]
        where[longest] = (where[longest] + shift) % array.shape[longest]
        spots.append(tuple(where))
    return array.at[spots[0]].set(least).at[spots[1]].set(top_value)


def setup_inputs(seed: int = 0) -> dict:
    key_list = jax.random.split(jax.random.key(seed), 6)
    gas = draw_gas(jax.random.fold_in(key_list[5], 71), 0)
    parcels = draw_parcels(jax.random.fold_in(key_list[5], 71), 0)
    home_cell_index = set_ends(jax.random.randint(key_list[2], (PACKET_ROOM, 128), 0, AXIAL_CELLS * CROSSWISE_CELLS * LATERAL_CELLS), jax.random.fold_in(key_list[2], 1), 0, (AXIAL_CELLS * CROSSWISE_CELLS * LATERAL_CELLS) - 1).astype(jnp.int32)
    order = jax.vmap(lambda own: jax.random.permutation(own, BLK_DEV))(jax.random.split(key_list[3], DEVICES)).reshape((DEVICES, BLK_DEV)).astype(jnp.int32)
    counts = draw_counts(jax.random.fold_in(key_list[5], 71), 0)
    return {"gas": gas, "parcels": parcels, "home_cell_index": home_cell_index, "order": order, "counts": counts}


GAMMA = 1.4
TIME_STEP = 0.1
RATE = 3.0
ACTIVATION = 2.0
HEAT = 5.0
DRAG_RELAX_TIME = 0.4
HEATING_RELAX = 0.6
EVAP_RATE = 1.5
LIQUID_HEAT = 2.0

def pressure_of(gas_state):
    motion_energy = gas_state[1] * gas_state[1] + gas_state[2] * gas_state[2] + gas_state[3] * gas_state[3]
    return (GAMMA - 1.0) * (gas_state[4] - 0.5 * motion_energy / gas_state[0])

def directional(column, direction):
    density = column[0]
    speed_along = column[1 + direction] / density
    pressure = pressure_of(column)
    pieces = [column[1 + direction], column[1] * speed_along, column[2] * speed_along, column[3] * speed_along, (column[4] + pressure) * speed_along, column[5] * speed_along]
    pieces[1 + direction] = pieces[1 + direction] + pressure
    return (jnp.stack(pieces), jnp.abs(speed_along) + jnp.sqrt(GAMMA * pressure / density))

def tendency(padded):
    interior = padded[:, 1:-1, 1:-1, 1:-1]
    result = jnp.zeros_like(interior)
    for direction in range(3):
        window = [slice(None), slice(1, -1), slice(1, -1), slice(1, -1)]
        window[direction + 1] = slice(None)
        column = padded[tuple(window)]
        fluxes, speeds = directional(column, direction)
        array_dim = direction + 1
        length = column.shape[array_dim]
        lower_flux = lax.slice_in_dim(fluxes, 0, length - 1, axis=array_dim)
        upper_flux = lax.slice_in_dim(fluxes, 1, length, axis=array_dim)
        lower_speed = lax.slice_in_dim(speeds, 0, length - 1, axis=direction)
        upper_speed = lax.slice_in_dim(speeds, 1, length, axis=direction)
        left_neighbor_fields = lax.slice_in_dim(column, 0, length - 1, axis=array_dim)
        upper_state = lax.slice_in_dim(column, 1, length, axis=array_dim)
        face_flux = 0.5 * (lower_flux + upper_flux) - 0.5 * jnp.maximum(lower_speed, upper_speed)[None] * (upper_state - left_neighbor_fields)
        result = result - (lax.slice_in_dim(face_flux, 1, length - 1, axis=array_dim) - lax.slice_in_dim(face_flux, 0, length - 2, axis=array_dim))
    burned = RATE * interior[5] * jnp.exp(-ACTIVATION * interior[0] / pressure_of(interior))
    result = result.at[4].add(HEAT * burned)
    result = result.at[5].add(-burned)
    return result

def parcel_update(parcels, transported):
    density = transported[0]
    gas_velocity = transported[1:4] / density
    gas_temp = pressure_of(transported) / density
    vapour = transported[5] / density
    drop_velocity = jnp.moveaxis(parcels[:, 0:3], 1, 0)
    drop_mass = parcels[:, 3]
    drop_temp = parcels[:, 4]
    root_mass = jnp.sqrt(drop_mass)
    new_mass = drop_mass * jnp.exp(-TIME_STEP * EVAP_RATE * gas_temp / (root_mass * (1.0 + vapour * vapour)))
    new_velocity = gas_velocity + (drop_velocity - gas_velocity) * jnp.exp(-TIME_STEP / (DRAG_RELAX_TIME * root_mass))
    new_temp = gas_temp + (drop_temp - gas_temp) * jnp.exp(-TIME_STEP / (HEATING_RELAX * root_mass))
    mass_source = drop_mass - new_mass
    momentum_source = drop_mass * drop_velocity - new_mass * new_velocity
    energy_source = 0.5 * (drop_mass * lax.optimization_barrier(jnp.sum(drop_velocity * drop_velocity, axis=0)) - new_mass * lax.optimization_barrier(jnp.sum(new_velocity * new_velocity, axis=0))) + LIQUID_HEAT * (drop_mass * drop_temp - new_mass * new_temp)
    sources = jnp.stack([mass_source, momentum_source[0], momentum_source[1], momentum_source[2], energy_source, mass_source])
    updated = jnp.stack([new_velocity[0], new_velocity[1], new_velocity[2], new_mass, new_temp], axis=1)
    return (updated, sources)

def pad_edges(field):
    return jnp.pad(field, ((0, 0), (1, 1), (1, 1), (1, 1)), mode='edge')

def reference(gas, parcels, home_cell_index, order, counts):
    section_one = gas + TIME_STEP * tendency(pad_edges(gas))
    stepped = 0.5 * gas + 0.5 * (section_one + TIME_STEP * tendency(pad_edges(section_one)))
    raveled_vapour_state = stepped.reshape(6, -1)
    group_numbers = jnp.arange(PACKET_ROOM, dtype=jnp.int32)
    owner = group_numbers // BLK_DEV
    slab_x = owner // (N_GY * N_GZ)
    block_slab_second = owner // N_GZ % N_GY
    slab_z = owner % N_GZ
    local_x = home_cell_index // (CROSSWISE_CELLS * LATERAL_CELLS)
    local_y = home_cell_index // LATERAL_CELLS % CROSSWISE_CELLS
    local_z = home_cell_index % LATERAL_CELLS
    domainwide_cell_number = ((slab_x[:, None] * AXIAL_CELLS + local_x) * NY + block_slab_second[:, None] * CROSSWISE_CELLS + local_y) * NZ + slab_z[:, None] * LATERAL_CELLS + local_z
    domainwide_cell_number = domainwide_cell_number.astype(jnp.int32)
    dev_ids = jnp.arange(DEVICES, dtype=jnp.int32)
    slot_ids = jnp.arange(BLK_DEV, dtype=jnp.int32)
    positions = jnp.zeros((DEVICES, BLK_DEV), jnp.int32).at[dev_ids[:, None], order].set(jnp.broadcast_to(slot_ids[None, :], (DEVICES, BLK_DEV)))
    kept = counts[:, 0]
    forward = counts[:, 1]
    backward = counts[:, 2]
    live_total = kept + forward + backward
    live = (positions.reshape(-1) < live_total[owner]).astype(jnp.float32)
    transported = raveled_vapour_state[:, domainwide_cell_number.reshape(-1)].reshape(6, PACKET_ROOM, 128)
    updated, sources = parcel_update(parcels, transported)
    sources = sources * live[None, :, None]
    gas_out = raveled_vapour_state.at[:, domainwide_cell_number.reshape(-1)].add(sources.reshape(6, -1)).reshape(6, NX, NY, NZ)
    stride = N_GY * N_GZ
    slab_dev = dev_ids // stride
    has_lower = slab_dev > 0
    has_upper = slab_dev < N_GX - 1
    lower_dev = jnp.where(has_lower, dev_ids - stride, dev_ids)
    upper_dev = jnp.where(has_upper, dev_ids + stride, dev_ids)
    from_lower = jnp.where(has_lower, forward[lower_dev], 0)
    from_upper = jnp.where(has_upper, backward[upper_dev], 0)
    slot_grid = slot_ids[None, :]
    own_count = kept[:, None]
    lower_count = from_lower[:, None]
    upper_count = from_upper[:, None]
    in_own = slot_grid < own_count
    in_lower = (slot_grid >= own_count) & (slot_grid < own_count + lower_count)
    in_upper = (slot_grid >= own_count + lower_count) & (slot_grid < own_count + lower_count + upper_count)
    source_dev = jnp.where(in_own, dev_ids[:, None], jnp.where(in_lower, lower_dev[:, None], upper_dev[:, None]))
    source_pos = jnp.where(in_own, slot_grid, jnp.where(in_lower, kept[lower_dev][:, None] + slot_grid - own_count, kept[upper_dev][:, None] + forward[upper_dev][:, None] + slot_grid - own_count - lower_count))
    source_pos = jnp.clip(source_pos, 0, BLK_DEV - 1).astype(jnp.int32)
    valid = (in_own | in_lower | in_upper).reshape(-1)
    source_slot = order[source_dev, source_pos]
    source_block = (source_dev * BLK_DEV + source_slot).reshape(-1).astype(jnp.int32)
    moved_parcels = jnp.where(valid[:, None, None], updated[source_block], 0.0)
    return (gas_out, moved_parcels)
```

```python
import functools

import jax
import jax.numpy as jnp
from jax import lax
from jax.experimental import pallas as pl
from jax.experimental.pallas import tpu as pltpu
from jax.sharding import PartitionSpec as P

GAMMA = 1.4
TIME_STEP = 0.1
RATE = 3.0
ACTIVATION = 2.0
HEAT = 5.0
DRAG_RELAX_TIME = 0.4
HEATING_RELAX = 0.6
EVAP_RATE = 1.5
LIQUID_HEAT = 2.0
AXES = ("gx", "gy", "gz")
MESH = pl.DeviceIdType.MESH
F32 = jnp.float32
BF16 = jnp.bfloat16


def pressure_of(u):
    motion_energy = u[1] * u[1] + u[2] * u[2] + u[3] * u[3]
    return (GAMMA - 1.0) * (u[4] - 0.5 * motion_energy / u[0])


def directional(u, k):
    inv = 1.0 / u[0]
    pressure = (GAMMA - 1.0) * (u[4] - 0.5 * inv * (u[1] * u[1] + u[2] * u[2] + u[3] * u[3]))
    along = u[1 + k] * inv
    flux = [u[1 + k], u[1] * along, u[2] * along, u[3] * along, (u[4] + pressure) * along, u[5] * along]
    flux[1 + k] = flux[1 + k] + pressure
    return flux, jnp.abs(along) + jnp.sqrt(GAMMA * pressure * inv)


def face(a, b):
    (ua, fa, sa), (ub, fb, sb) = a, b
    top = jnp.maximum(sa, sb)
    return [0.5 * (fa[c] + fb[c]) - 0.5 * top * (ub[c] - ua[c]) for c in range(6)]


def pack_faces(u, faces):
    planes, rows, lanes = u[0].shape
    plane_id = lax.broadcasted_iota(jnp.int32, (planes, rows, lanes), 0)
    lane_id = lax.broadcasted_iota(jnp.int32, (planes, rows, lanes), 2)
    here = plane_id == lane_id
    for c in range(6):
        faces[0, 0, c] = u[c][0]
        faces[0, 1, c] = u[c][planes - 1]
        faces[1, 0, c] = u[c][:, 0, :]
        faces[1, 1, c] = u[c][:, rows - 1, :]
        for side, lane in ((0, 0), (1, lanes - 1)):
            column = jnp.broadcast_to(u[c][:, :, lane : lane + 1], (planes, rows, lanes))
            column = jnp.where(here | ((plane_id == 0) & (lane_id >= planes)), column, 0.0)
            faces[2, side, c] = jnp.sum(column, axis=0)


def tendency(u, faces, ghosts):
    shape = u[0].shape
    planes, rows, lanes = shape
    row_id = lax.broadcasted_iota(jnp.int32, shape, 1)
    lane_id = lax.broadcasted_iota(jnp.int32, shape, 2)
    result = [None] * 6

    def edge_faces(k):
        own = [[faces[k, side, c] for c in range(6)] for side in range(2)]
        out = [[ghosts[k, side, c] for c in range(6)] for side in range(2)]
        state = lambda v: (v,) + directional(v, k)
        return face(state(out[0]), state(own[0])), face(state(own[1]), state(out[1]))

    for k in range(3):
        low, high = edge_faces(k)
        flux, speed = directional(u, k)
        if k == 0:
            a = ([v[:-1] for v in u], [v[:-1] for v in flux], speed[:-1])
            b = ([v[1:] for v in u], [v[1:] for v in flux], speed[1:])
            inner = face(a, b)
            for c in range(6):
                h = jnp.concatenate([low[c][None], inner[c], high[c][None]], axis=0)
                result[c] = h[:-1] - h[1:]
            continue
        axis, length = k, shape[k]
        place = row_id if k == 1 else lane_id
        ahead = lambda v: pltpu.roll(v, length - 1, axis)
        inner = face((u, flux, speed), ([ahead(v) for v in u], [ahead(v) for v in flux], ahead(speed)))
        for c in range(6):
            if k == 1:
                lo = jnp.broadcast_to(low[c][:, None, :], shape)
                hi = jnp.broadcast_to(high[c][:, None, :], shape)
            else:
                lo = jnp.stack([jnp.broadcast_to(low[c][:, x : x + 1], (rows, lanes)) for x in range(planes)])
                hi = jnp.stack([jnp.broadcast_to(high[c][:, x : x + 1], (rows, lanes)) for x in range(planes)])
            upper = jnp.where(place == length - 1, hi, inner[c])
            lower = jnp.where(place == 0, lo, pltpu.roll(inner[c], 1, axis))
            result[c] = result[c] + (lower - upper)
    burned = RATE * u[5] * jnp.exp(-ACTIVATION * u[0] / pressure_of(u))
    result[4] = result[4] + HEAT * burned
    result[5] = result[5] - burned
    return result


def parcel_update(drop, gas):
    inv = 1.0 / gas[0]
    gas_velocity = [gas[1] * inv, gas[2] * inv, gas[3] * inv]
    gas_temp = pressure_of(gas) * inv
    vapour = gas[5] * inv
    mass, temp = drop[3], drop[4]
    root = jnp.sqrt(mass)
    inv_root = 1.0 / root
    new_mass = mass * jnp.exp(-TIME_STEP * EVAP_RATE * gas_temp * inv_root / (1.0 + vapour * vapour))
    drag = jnp.exp((-TIME_STEP / DRAG_RELAX_TIME) * inv_root)
    warm = jnp.exp((-TIME_STEP / HEATING_RELAX) * inv_root)
    new_velocity = [gas_velocity[d] + (drop[d] - gas_velocity[d]) * drag for d in range(3)]
    new_temp = gas_temp + (temp - gas_temp) * warm
    lost = mass - new_mass
    momentum = [mass * drop[d] - new_mass * new_velocity[d] for d in range(3)]
    before = drop[0] * drop[0] + drop[1] * drop[1] + drop[2] * drop[2]
    after = new_velocity[0] * new_velocity[0] + new_velocity[1] * new_velocity[1] + new_velocity[2] * new_velocity[2]
    energy = 0.5 * (mass * before - new_mass * after) + LIQUID_HEAT * (mass * temp - new_mass * new_temp)
    return new_velocity + [new_mass, new_temp], [lost] + momentum + [energy]


def split_two(v):
    head = v.astype(BF16)
    return head, (v - head.astype(F32)).astype(BF16)


def kernel(
    sizes, order_s, counts_s, order_v, gas, parcels, cells,
    gas_out, moved,
    faces, ghosts, stepped, table, hot, high_id, carried, live, spread, total,
    updated, going, coming, count_out, count_in,
    face_send, face_recv, move_send, move_recv, count_send, count_recv,
):
    place = [lax.axis_index(a) for a in AXES]
    planes, rows, lanes = gas.shape[1:]
    slots = parcels.shape[0]
    cap = slots // 4
    group = 8
    chunks = slots // group
    half = planes // 2
    wide = half * rows
    kept, forward, backward = counts_s[0, 0], counts_s[0, 1], counts_s[0, 2]

    def has(k, side):
        return place[k] > 0 if side == 0 else place[k] < sizes[k] - 1

    def neighbour(k, side):
        return {AXES[k]: lax.rem(place[k] + (sizes[k] - 1 if side == 0 else 1), sizes[k])}

    def copy_to(k, side, src, dst, send, recv):
        return pltpu.make_async_remote_copy(
            src_ref=src, dst_ref=dst, send_sem=send, recv_sem=recv,
            device_id=neighbour(k, side), device_id_type=MESH,
        )

    def face_copy(turn, k, side):
        return copy_to(
            k, side, faces.at[turn, k, side], ghosts.at[turn, k, 1 - side],
            face_send.at[turn, k, side], face_recv.at[turn, k, 1 - side],
        )

    def count_copy(side):
        return copy_to(0, side, count_out.at[side], count_in.at[1 - side], count_send.at[side], count_recv.at[1 - side])

    def move_copy(side):
        return copy_to(0, side, going.at[side], coming.at[1 - side], move_send.at[side], move_recv.at[1 - side])

    links = [(k, side) for k in range(3) for side in range(2) if sizes[k] > 1]

    barrier = pltpu.get_barrier_semaphore()
    arrivals = 0
    for k, side in links:
        @pl.when(has(k, side))
        def _():
            pl.semaphore_signal(barrier, inc=1, device_id=neighbour(k, side), device_id_type=MESH)
        arrivals = arrivals + has(k, side).astype(jnp.int32)

    u = [gas[c] for c in range(6)]
    pack_faces(u, faces.at[0])
    count_out[0] = jnp.full(count_out.shape[1:], backward, jnp.int32)
    count_out[1] = jnp.full(count_out.shape[1:], forward, jnp.int32)
    for side in range(2):
        @pl.when(jnp.logical_not(has(0, side)))
        def _():
            count_in[side] = jnp.zeros(count_in.shape[1:], jnp.int32)
            coming[side] = jnp.zeros(coming.shape[1:], F32)

    pl.semaphore_wait(barrier, arrivals)

    def send_faces(turn):
        for k in range(3):
            for side in range(2):
                if (k, side) in links:
                    @pl.when(has(k, side))
                    def _():
                        face_copy(turn, k, side).start()

                @pl.when(jnp.logical_not(has(k, side)))
                def _():
                    ghosts[turn, k, side] = faces[turn, k, side]

    def receive_faces(turn):
        for k, side in links:
            @pl.when(has(k, side))
            def _():
                face_copy(turn, k, 1 - side).wait_recv()

    send_faces(0)
    for side in range(2):
        if sizes[0] > 1:
            @pl.when(has(0, side))
            def _():
                count_copy(side).start()

    def build(i, carry):
        cell = cells[pl.ds(i * group, group), :]
        column = (cell % lanes) + (cell // (lanes * wide)) * lanes
        high_id[pl.ds(i * group, group), :] = (cell // lanes) % wide
        column_id = lax.broadcasted_iota(jnp.int32, (2 * lanes, lanes), 0)
        for j in range(group):
            match = column_id == column[j : j + 1, :]
            hot[i, :, j * lanes : (j + 1) * lanes] = jnp.where(match, 1.0, 0.0).astype(BF16)
        return carry

    lax.fori_loop(0, chunks // 2, build, 0)
    receive_faces(0)
    change = tendency(u, faces.at[0], ghosts.at[0])
    one = [u[c] + TIME_STEP * change[c] for c in range(6)]
    pack_faces(one, faces.at[1])
    send_faces(1)
    for c in range(6):
        stepped[c] = one[c]

    lax.fori_loop(chunks // 2, chunks, build, 0)
    slot_id = lax.broadcasted_iota(jnp.int32, (slots, slots), 0)
    turn_id = lax.broadcasted_iota(jnp.int32, (slots, slots), 1)
    used = (order_v[...] == slot_id) & (turn_id < kept + forward + backward)
    used = jnp.sum(jnp.where(used, 1.0, 0.0), axis=1, keepdims=True)
    live[...] = jnp.broadcast_to(used, live.shape)

    receive_faces(1)
    one = [stepped[c] for c in range(6)]
    change = tendency(one, faces.at[1], ghosts.at[1])
    for c in range(6):
        v = 0.5 * gas[c] + 0.5 * (one[c] + TIME_STEP * change[c])
        stepped[c] = v
        for part in range(2):
            head, rest = split_two(v[part * half : (part + 1) * half].reshape(wide, lanes))
            table[c * wide : (c + 1) * wide, part * lanes : (part + 1) * lanes] = head
            table[(6 + c) * wide : (7 + c) * wide, part * lanes : (part + 1) * lanes] = rest

    def gather(i, carry):
        got = jnp.dot(table[...], hot[i], preferred_element_type=F32)
        row_of = high_id[pl.ds(i * group, group), :]
        row_id = lax.broadcasted_iota(jnp.int32, (wide, lanes), 0)
        for j in range(group):
            match = row_id == row_of[j : j + 1, :]
            for c in range(6):
                here = slice(j * lanes, (j + 1) * lanes)
                both = got[c * wide : (c + 1) * wide, here] + got[(6 + c) * wide : (7 + c) * wide, here]
                carried[i, c, j : j + 1, :] = jnp.sum(jnp.where(match, both, 0.0), axis=0, keepdims=True)
        block = pl.ds(i * group, group)
        drop = [parcels[block, d, :] for d in range(5)]
        new, source = parcel_update(drop, [carried[i, c] for c in range(6)])
        for d in range(5):
            updated[block, d, :] = new[d]
        for c in range(5):
            carried[i, c] = source[c] * live[block, :]
        return carry

    lax.fori_loop(0, chunks, gather, 0)

    def choose(i, carry):
        going[1, i] = updated[order_s[0, kept + i]]
        going[0, i] = updated[order_s[0, kept + forward + i]]
        return carry

    lax.fori_loop(0, cap, choose, 0)
    for side in range(2):
        if sizes[0] > 1:
            @pl.when(has(0, side))
            def _():
                move_copy(side).start()

    total[...] = jnp.zeros_like(total)

    def scatter(i, carry):
        row_of = high_id[pl.ds(i * group, group), :]
        row_id = lax.broadcasted_iota(jnp.int32, (wide, lanes), 0)
        source = [carried[i, c] for c in range(5)]
        head = [v.astype(BF16).astype(F32) for v in source]
        rest = [v - h for v, h in zip(source, head)]
        for j in range(group):
            match = row_id == row_of[j : j + 1, :]
            for c, v in enumerate(head + rest):
                spread[c * wide : (c + 1) * wide, j * lanes : (j + 1) * lanes] = jnp.where(
                    match, v[j : j + 1, :], 0.0
                ).astype(BF16)
        total[...] += lax.dot_general(
            spread[...], hot[i], (((1,), (1,)), ((), ())), preferred_element_type=F32
        )
        return carry

    lax.fori_loop(0, chunks, scatter, 0)
    for c in range(6):
        s = 0 if c == 5 else c
        summed = total[s * wide : (s + 1) * wide, :] + total[(5 + s) * wide : (6 + s) * wide, :]
        for part in range(2):
            part_sum = summed[:, part * lanes : (part + 1) * lanes].reshape(half, rows, lanes)
            here = slice(part * half, (part + 1) * half)
            gas_out[c, here] = stepped[c, here] + part_sum

    for side in range(2):
        if sizes[0] > 1:
            @pl.when(has(0, side))
            def _():
                count_copy(1 - side).wait_recv()
                move_copy(1 - side).wait_recv()

    lower = count_in[0][0, 0]
    upper = count_in[1][0, 0]

    def place_block(j, carry):
        own = updated[order_s[0, j]]
        below = coming[0, jnp.clip(j - kept, 0, cap - 1)]
        above = coming[1, jnp.clip(j - kept - lower, 0, cap - 1)]
        far = jnp.where(j < kept + lower, below, jnp.where(j < kept + lower + upper, above, 0.0))
        moved[j] = jnp.where(j < kept, own, far)
        return carry

    lax.fori_loop(0, slots, place_block, 0)

    for turn in range(2):
        for k, side in links:
            @pl.when(has(k, side))
            def _():
                face_copy(turn, k, side).wait_send()
    for side in range(2):
        if sizes[0] > 1:
            @pl.when(has(0, side))
            def _():
                count_copy(side).wait_send()
                move_copy(side).wait_send()


def body(sizes, gas, parcels, home_cell_index, order, counts):
    planes, rows, lanes = gas.shape[1:]
    slots = parcels.shape[0]
    group = 8
    wide = planes // 2 * rows
    cap = slots // 4
    vmem = pl.BlockSpec(memory_space=pltpu.VMEM)
    smem = pl.BlockSpec(memory_space=pltpu.SMEM)
    dma = pltpu.SemaphoreType.DMA
    return pl.pallas_call(
        functools.partial(kernel, sizes),
        out_shape=(
            jax.ShapeDtypeStruct(gas.shape, F32),
            jax.ShapeDtypeStruct(parcels.shape, F32),
        ),
        in_specs=[smem, smem, vmem, vmem, vmem, vmem],
        out_specs=(vmem, vmem),
        scratch_shapes=[
            pltpu.VMEM((2, 3, 2, 6, rows, lanes), F32),
            pltpu.VMEM((2, 3, 2, 6, rows, lanes), F32),
            pltpu.VMEM(gas.shape, F32),
            pltpu.VMEM((12 * wide, 2 * lanes), BF16),
            pltpu.VMEM((slots // group, 2 * lanes, group * lanes), BF16),
            pltpu.VMEM((slots, lanes), jnp.int32),
            pltpu.VMEM((slots // group, 6, group, lanes), F32),
            pltpu.VMEM((slots, lanes), F32),
            pltpu.VMEM((10 * wide, group * lanes), BF16),
            pltpu.VMEM((10 * wide, 2 * lanes), F32),
            pltpu.VMEM(parcels.shape, F32),
            pltpu.VMEM((2, cap) + parcels.shape[1:], F32),
            pltpu.VMEM((2, cap) + parcels.shape[1:], F32),
            pltpu.VMEM((2, 8, lanes), jnp.int32),
            pltpu.VMEM((2, 8, lanes), jnp.int32),
            dma((2, 3, 2)), dma((2, 3, 2)), dma((2,)), dma((2,)), dma((2,)), dma((2,)),
        ],
        compiler_params=pltpu.CompilerParams(
            collective_id=0, has_side_effects=True, vmem_limit_bytes=48 * 1024 * 1024
        ),
    )(order, counts, order, gas, parcels, home_cell_index)


def solution(mesh):
    in_specs = (
        P(None, "gx", "gy", "gz"),
        P(("gx", "gy", "gz"), None, None),
        P(("gx", "gy", "gz"), None),
        P(("gx", "gy", "gz"), None),
        P(("gx", "gy", "gz"), None),
    )
    out_specs = (P(None, "gx", "gy", "gz"), P(("gx", "gy", "gz"), None, None))
    sizes = tuple(mesh.shape[a] for a in AXES)
    return jax.shard_map(
        functools.partial(body, sizes), mesh=mesh, in_specs=in_specs, out_specs=out_specs, check_vma=False
    )
```

```python
import functools

import jax
import jax.numpy as jnp
from jax import lax
from jax.experimental import pallas as pl
from jax.experimental.pallas import tpu as pltpu
from jax.sharding import PartitionSpec as P

GAMMA = 1.4
TIME_STEP = 0.1
RATE = 3.0
ACTIVATION = 2.0
HEAT = 5.0
DRAG_RELAX_TIME = 0.4
HEATING_RELAX = 0.6
EVAP_RATE = 1.5
LIQUID_HEAT = 2.0
AXES = ("gx", "gy", "gz")
MESH = pl.DeviceIdType.MESH
F32 = jnp.float32
BF16 = jnp.bfloat16


def pressure_of(u):
    motion_energy = u[1] * u[1] + u[2] * u[2] + u[3] * u[3]
    return (GAMMA - 1.0) * (u[4] - 0.5 * motion_energy / u[0])


def directional(u, k):
    inv = 1.0 / u[0]
    pressure = (GAMMA - 1.0) * (u[4] - 0.5 * inv * (u[1] * u[1] + u[2] * u[2] + u[3] * u[3]))
    along = u[1 + k] * inv
    flux = [u[1 + k], u[1] * along, u[2] * along, u[3] * along, (u[4] + pressure) * along, u[5] * along]
    flux[1 + k] = flux[1 + k] + pressure
    return flux, jnp.abs(along) + jnp.sqrt(GAMMA * pressure * inv)


def face(a, b):
    (ua, fa, sa), (ub, fb, sb) = a, b
    top = jnp.maximum(sa, sb)
    return [0.5 * (fa[c] + fb[c]) - 0.5 * top * (ub[c] - ua[c]) for c in range(6)]


def pack_faces(ref, faces):
    planes, rows, lanes = ref.shape[1:]
    plane_id = lax.broadcasted_iota(jnp.int32, (planes, rows, lanes), 0)
    lane_id = lax.broadcasted_iota(jnp.int32, (planes, rows, lanes), 2)
    here = plane_id == lane_id
    for c in range(6):
        faces[0, 0, c] = ref[c, 0]
        faces[0, 1, c] = ref[c, planes - 1]
        faces[1, 0, c] = ref[c, :, 0, :]
        faces[1, 1, c] = ref[c, :, rows - 1, :]
        whole = ref[c]
        for side, lane in ((0, 0), (1, lanes - 1)):
            column = jnp.broadcast_to(whole[:, :, lane : lane + 1], (planes, rows, lanes))
            column = jnp.where(here | ((plane_id == 0) & (lane_id >= planes)), column, 0.0)
            faces[2, side, c] = jnp.sum(column, axis=0)


def tendency(u, faces, ghosts):
    shape = u[0].shape
    planes, rows, lanes = shape
    row_id = lax.broadcasted_iota(jnp.int32, shape, 1)
    lane_id = lax.broadcasted_iota(jnp.int32, shape, 2)
    result = [None] * 6

    def edge_faces(k):
        own = [[faces[k, side, c] for c in range(6)] for side in range(2)]
        out = [[ghosts[k, side, c] for c in range(6)] for side in range(2)]
        state = lambda v: (v,) + directional(v, k)
        return face(state(out[0]), state(own[0])), face(state(own[1]), state(out[1]))

    for k in range(3):
        low, high = edge_faces(k)
        flux, speed = directional(u, k)
        if k == 0:
            a = ([v[:-1] for v in u], [v[:-1] for v in flux], speed[:-1])
            b = ([v[1:] for v in u], [v[1:] for v in flux], speed[1:])
            inner = face(a, b)
            for c in range(6):
                h = jnp.concatenate([low[c][None], inner[c], high[c][None]], axis=0)
                result[c] = h[:-1] - h[1:]
            continue
        axis, length = k, shape[k]
        place = row_id if k == 1 else lane_id
        ahead = lambda v: pltpu.roll(v, length - 1, axis)
        inner = face((u, flux, speed), ([ahead(v) for v in u], [ahead(v) for v in flux], ahead(speed)))
        for c in range(6):
            if k == 1:
                lo = jnp.broadcast_to(low[c][:, None, :], shape)
                hi = jnp.broadcast_to(high[c][:, None, :], shape)
            else:
                lo = jnp.stack([jnp.broadcast_to(low[c][:, x : x + 1], (rows, lanes)) for x in range(planes)])
                hi = jnp.stack([jnp.broadcast_to(high[c][:, x : x + 1], (rows, lanes)) for x in range(planes)])
            upper = jnp.where(place == length - 1, hi, inner[c])
            lower = jnp.where(place == 0, lo, pltpu.roll(inner[c], 1, axis))
            result[c] = result[c] + (lower - upper)
    burned = RATE * u[5] * jnp.exp(-ACTIVATION * u[0] / pressure_of(u))
    result[4] = result[4] + HEAT * burned
    result[5] = result[5] - burned
    return result


def parcel_update(drop, gas):
    inv = 1.0 / gas[0]
    gas_velocity = [gas[1] * inv, gas[2] * inv, gas[3] * inv]
    gas_temp = pressure_of(gas) * inv
    vapour = gas[5] * inv
    mass, temp = drop[3], drop[4]
    root = jnp.sqrt(mass)
    inv_root = 1.0 / root
    new_mass = mass * jnp.exp(-TIME_STEP * EVAP_RATE * gas_temp * inv_root / (1.0 + vapour * vapour))
    drag = jnp.exp((-TIME_STEP / DRAG_RELAX_TIME) * inv_root)
    warm = jnp.exp((-TIME_STEP / HEATING_RELAX) * inv_root)
    new_velocity = [gas_velocity[d] + (drop[d] - gas_velocity[d]) * drag for d in range(3)]
    new_temp = gas_temp + (temp - gas_temp) * warm
    lost = mass - new_mass
    momentum = [mass * drop[d] - new_mass * new_velocity[d] for d in range(3)]
    before = drop[0] * drop[0] + drop[1] * drop[1] + drop[2] * drop[2]
    after = new_velocity[0] * new_velocity[0] + new_velocity[1] * new_velocity[1] + new_velocity[2] * new_velocity[2]
    energy = 0.5 * (mass * before - new_mass * after) + LIQUID_HEAT * (mass * temp - new_mass * new_temp)
    return new_velocity + [new_mass, new_temp], [lost] + momentum + [energy]


def split_three(v):
    head = v.astype(BF16)
    rest = v - head.astype(F32)
    middle = rest.astype(BF16)
    return head, middle, (rest - middle.astype(F32)).astype(BF16)


def kernel(
    sizes, counts_s, order_v, gas, parcels, cells,
    gas_out, moved,
    faces, ghosts, stepped, hot, high_hot, sources, live, spread, total,
    choice, blocks, own_blocks, going, coming, arrived, count_out, count_in,
    face_send, face_recv, move_send, move_recv, count_send, count_recv,
):
    place = [lax.axis_index(a) for a in AXES]
    planes, rows, lanes = gas.shape[1:]
    slots = parcels.shape[1]
    cap = slots // 4
    group = 8
    chunks = slots // group
    half = planes // 2
    wide = half * rows
    kept, forward, backward = counts_s[0, 0], counts_s[0, 1], counts_s[0, 2]

    def has(k, side):
        return place[k] > 0 if side == 0 else place[k] < sizes[k] - 1

    def neighbour(k, side):
        return {AXES[k]: lax.rem(place[k] + (sizes[k] - 1 if side == 0 else 1), sizes[k])}

    def copy_to(k, side, src, dst, send, recv):
        return pltpu.make_async_remote_copy(
            src_ref=src, dst_ref=dst, send_sem=send, recv_sem=recv,
            device_id=neighbour(k, side), device_id_type=MESH,
        )

    def face_copy(turn, k, side):
        return copy_to(
            k, side, faces.at[turn, k, side], ghosts.at[turn, k, 1 - side],
            face_send.at[turn, k, side], face_recv.at[turn, k, 1 - side],
        )

    def count_copy(side):
        return copy_to(0, side, count_out.at[side], count_in.at[1 - side], count_send.at[side], count_recv.at[1 - side])

    def move_copy(side):
        return copy_to(0, side, going.at[side], coming.at[1 - side], move_send.at[side], move_recv.at[1 - side])

    links = [(k, side) for k in range(3) for side in range(2) if sizes[k] > 1]

    barrier = pltpu.get_barrier_semaphore()
    arrivals = 0
    for k, side in links:
        @pl.when(has(k, side))
        def _():
            pl.semaphore_signal(barrier, inc=1, device_id=neighbour(k, side), device_id_type=MESH)
        arrivals = arrivals + has(k, side).astype(jnp.int32)

    u = [gas[c] for c in range(6)]
    pack_faces(gas, faces.at[0])
    count_out[0] = jnp.full(count_out.shape[1:], backward, jnp.int32)
    count_out[1] = jnp.full(count_out.shape[1:], forward, jnp.int32)
    for side in range(2):
        @pl.when(jnp.logical_not(has(0, side)))
        def _():
            count_in[side] = jnp.zeros(count_in.shape[1:], jnp.int32)
            coming[side] = jnp.zeros(coming.shape[1:], F32)

    pl.semaphore_wait(barrier, arrivals)

    def send_faces(turn):
        for k in range(3):
            for side in range(2):
                if (k, side) in links:
                    @pl.when(has(k, side))
                    def _():
                        face_copy(turn, k, side).start()

                @pl.when(jnp.logical_not(has(k, side)))
                def _():
                    ghosts[turn, k, side] = faces[turn, k, side]

    def receive_faces(turn):
        for k, side in links:
            @pl.when(has(k, side))
            def _():
                face_copy(turn, k, 1 - side).wait_recv()

    send_faces(0)
    for side in range(2):
        if sizes[0] > 1:
            @pl.when(has(0, side))
            def _():
                count_copy(side).start()

    def build(i, carry):
        cell = cells[pl.ds(i * group, group), :]
        column = (cell % lanes) + (cell // (lanes * wide)) * lanes
        high = (cell // lanes) % wide
        column = column.astype(F32).T
        column_id = lax.broadcasted_iota(jnp.int32, (lanes, 2 * lanes), 1).astype(F32)
        row_id = lax.broadcasted_iota(jnp.int32, (wide, lanes), 0)
        for j in range(group):
            here = slice(j * lanes, (j + 1) * lanes)
            match = jnp.broadcast_to(column[:, j : j + 1], column_id.shape) == column_id
            hot[i, here, :] = jnp.where(match, 1.0, 0.0).astype(BF16)
            high_hot[i, :, here] = jnp.where(row_id == high[j : j + 1, :], 1.0, 0.0).astype(BF16)
        return carry

    lax.fori_loop(0, chunks // 2, build, 0)
    receive_faces(0)
    change = tendency(u, faces.at[0], ghosts.at[0])
    one = [u[c] + TIME_STEP * change[c] for c in range(6)]
    for c in range(6):
        stepped[c] = one[c]
    pack_faces(stepped, faces.at[1])
    send_faces(1)

    lax.fori_loop(chunks // 2, chunks, build, 0)
    slot_id = lax.broadcasted_iota(jnp.int32, (slots, slots), 0)
    turn_id = lax.broadcasted_iota(jnp.int32, (slots, slots), 1)
    used = (order_v[...] == slot_id) & (turn_id < kept + forward + backward)
    used = jnp.sum(jnp.where(used, 1.0, 0.0), axis=1, keepdims=True)
    live[...] = jnp.broadcast_to(used, live.shape)

    rows_out = slots + 2 * cap
    take_id = lax.broadcasted_iota(jnp.int32, (rows_out, slots), 0)
    from_id = lax.broadcasted_iota(jnp.int32, (rows_out, slots), 1)
    spot = jnp.where(take_id < slots, take_id, take_id - slots + kept)
    spot = jnp.where(take_id < slots + cap, spot, take_id - slots - cap + kept + forward)
    origin = jnp.where(from_id == spot, order_v[...].astype(F32), 0.0)
    origin = jnp.sum(origin, axis=1, keepdims=True)
    wide_id = lax.broadcasted_iota(jnp.int32, choice.shape, 1) % slots
    take_id = lax.broadcasted_iota(jnp.int32, choice.shape, 0)
    chosen = (wide_id.astype(F32) == origin) & ((take_id < kept) | (take_id >= slots))
    choice[...] = jnp.where(chosen, 1.0, 0.0).astype(BF16)

    receive_faces(1)
    one = [stepped[c] for c in range(6)]
    change = tendency(one, faces.at[1], ghosts.at[1])
    for c in range(6):
        v = 0.5 * gas[c] + 0.5 * (one[c] + TIME_STEP * change[c])
        stepped[c] = v

    def gather(i, carry):
        block = pl.ds(i * group, group)
        cell = cells[block, :]
        lane, high = cell % lanes, cell // lanes
        got = [jnp.zeros((group, lanes), F32)] * 6
        for x in range(planes):
            for y in range(rows):
                match = high == x * rows + y
                for c in range(6):
                    row = jnp.broadcast_to(stepped[c, x, y : y + 1, :], (group, lanes))
                    value = jnp.take_along_axis(row, lane, axis=1, mode="promise_in_bounds")
                    got[c] = jnp.where(match, value, got[c])
        new, source = parcel_update([parcels[d, block, :] for d in range(5)], got)
        for d in range(5):
            for part, term in enumerate(split_three(new[d])):
                blocks[d, pl.ds(part * slots + i * group, group), :] = term.astype(F32)
        for c in range(5):
            sources[i, c] = source[c] * live[block, :]
        return carry

    lax.fori_loop(0, chunks, gather, 0)

    for d in range(5):
        sorted_blocks = jnp.dot(choice[...], blocks[d].astype(BF16), preferred_element_type=F32)
        own_blocks[d] = sorted_blocks[:slots]
        going[1, d] = sorted_blocks[slots : slots + cap]
        going[0, d] = sorted_blocks[slots + cap :]
    for side in range(2):
        if sizes[0] > 1:
            @pl.when(has(0, side))
            def _():
                move_copy(side).start()

    total[...] = jnp.zeros_like(total)

    def scatter(i, carry):
        source = [sources[i, c] for c in range(5)]
        head = [v.astype(BF16).astype(F32) for v in source]
        rest = [v - h for v, h in zip(source, head)]
        for j in range(group):
            here = slice(j * lanes, (j + 1) * lanes)
            match = high_hot[i, :, here]
            for c, v in enumerate(head + rest):
                term = jnp.broadcast_to(v[j : j + 1, :], (wide, lanes)).astype(BF16)
                spread[c * wide : (c + 1) * wide, here] = match * term
        total[...] += jnp.dot(spread[...], hot[i], preferred_element_type=F32)
        return carry

    lax.fori_loop(0, chunks, scatter, 0)
    for c in range(6):
        s = 0 if c == 5 else c
        summed = total[s * wide : (s + 1) * wide, :] + total[(5 + s) * wide : (6 + s) * wide, :]
        for part in range(2):
            part_sum = summed[:, part * lanes : (part + 1) * lanes].reshape(half, rows, lanes)
            here = slice(part * half, (part + 1) * half)
            gas_out[c, here] = stepped[c, here] + part_sum

    for side in range(2):
        if sizes[0] > 1:
            @pl.when(has(0, side))
            def _():
                count_copy(1 - side).wait_recv()
                move_copy(1 - side).wait_recv()

    place_shape = (slots, 6 * cap)
    slot_id = lax.broadcasted_iota(jnp.int32, place_shape, 0)
    block_id = lax.broadcasted_iota(jnp.int32, place_shape, 1) % (2 * cap)
    lower = jnp.broadcast_to(count_in[0, 0:1, : 6 * cap], place_shape)
    upper = jnp.broadcast_to(count_in[1, 0:1, : 6 * cap], place_shape)
    from_lower = (slot_id - kept == block_id) & (block_id < cap) & (block_id < lower)
    above = block_id - cap
    from_upper = (slot_id - kept - lower == above) & (above >= 0) & (above < upper)
    fill = jnp.where(from_lower | from_upper, 1.0, 0.0).astype(BF16)
    for d in range(5):
        for side in range(2):
            for part, term in enumerate(split_three(coming[side, d])):
                start = part * 2 * cap + side * cap
                arrived[d, start : start + cap, :] = term
        moved[d] = own_blocks[d] + jnp.dot(fill, arrived[d], preferred_element_type=F32)

    for turn in range(2):
        for k, side in links:
            @pl.when(has(k, side))
            def _():
                face_copy(turn, k, side).wait_send()
    for side in range(2):
        if sizes[0] > 1:
            @pl.when(has(0, side))
            def _():
                count_copy(side).wait_send()
                move_copy(side).wait_send()


def body(sizes, gas, parcels, home_cell_index, order, counts):
    planes, rows, lanes = gas.shape[1:]
    parcels = jnp.transpose(parcels, (1, 0, 2))
    slots = parcels.shape[1]
    group = 8
    chunks = slots // group
    wide = planes // 2 * rows
    cap = slots // 4
    vmem = pl.BlockSpec(memory_space=pltpu.VMEM)
    smem = pl.BlockSpec(memory_space=pltpu.SMEM)
    dma = pltpu.SemaphoreType.DMA
    gas_out, moved = pl.pallas_call(
        functools.partial(kernel, sizes),
        out_shape=(
            jax.ShapeDtypeStruct(gas.shape, F32),
            jax.ShapeDtypeStruct(parcels.shape, F32),
        ),
        in_specs=[smem, vmem, vmem, vmem, vmem],
        out_specs=(vmem, vmem),
        scratch_shapes=[
            pltpu.VMEM((2, 3, 2, 6, rows, lanes), F32),
            pltpu.VMEM((2, 3, 2, 6, rows, lanes), F32),
            pltpu.VMEM(gas.shape, F32),
            pltpu.VMEM((chunks, group * lanes, 2 * lanes), BF16),
            pltpu.VMEM((chunks, wide, group * lanes), BF16),
            pltpu.VMEM((chunks, 5, group, lanes), F32),
            pltpu.VMEM((slots, lanes), F32),
            pltpu.VMEM((10 * wide, group * lanes), BF16),
            pltpu.VMEM((10 * wide, 2 * lanes), F32),
            pltpu.VMEM((slots + 2 * cap, 3 * slots), BF16),
            pltpu.VMEM((5, 3 * slots, lanes), F32),
            pltpu.VMEM(parcels.shape, F32),
            pltpu.VMEM((2, 5, cap, lanes), F32),
            pltpu.VMEM((2, 5, cap, lanes), F32),
            pltpu.VMEM((5, 6 * cap, lanes), BF16),
            pltpu.VMEM((2, 8, lanes), jnp.int32),
            pltpu.VMEM((2, 8, lanes), jnp.int32),
            dma((2, 3, 2)), dma((2, 3, 2)), dma((2,)), dma((2,)), dma((2,)), dma((2,)),
        ],
        compiler_params=pltpu.CompilerParams(
            collective_id=0, has_side_effects=True, vmem_limit_bytes=48 * 1024 * 1024
        ),
    )(counts, order, gas, parcels, home_cell_index)
    return gas_out, jnp.transpose(moved, (1, 0, 2))


def solution(mesh):
    in_specs = (
        P(None, "gx", "gy", "gz"),
        P(("gx", "gy", "gz"), None, None),
        P(("gx", "gy", "gz"), None),
        P(("gx", "gy", "gz"), None),
        P(("gx", "gy", "gz"), None),
    )
    out_specs = (P(None, "gx", "gy", "gz"), P(("gx", "gy", "gz"), None, None))
    sizes = tuple(mesh.shape[a] for a in AXES)
    return jax.shard_map(
        functools.partial(body, sizes), mesh=mesh, in_specs=in_specs, out_specs=out_specs, check_vma=False
    )
```

```python
import functools

import jax
import jax.numpy as jnp
from jax import lax
from jax.experimental import pallas as pl
from jax.experimental.pallas import tpu as pltpu
from jax.sharding import PartitionSpec as P

GAMMA = 1.4
TIME_STEP = 0.1
RATE = 3.0
ACTIVATION = 2.0
HEAT = 5.0
DRAG_RELAX_TIME = 0.4
HEATING_RELAX = 0.6
EVAP_RATE = 1.5
LIQUID_HEAT = 2.0
AXES = ("gx", "gy", "gz")
MESH = pl.DeviceIdType.MESH
F32 = jnp.float32
BF16 = jnp.bfloat16


def pressure_of(u):
    motion_energy = u[1] * u[1] + u[2] * u[2] + u[3] * u[3]
    return (GAMMA - 1.0) * (u[4] - 0.5 * motion_energy / u[0])


def directional(u, k):
    inv = 1.0 / u[0]
    pressure = (GAMMA - 1.0) * (u[4] - 0.5 * inv * (u[1] * u[1] + u[2] * u[2] + u[3] * u[3]))
    along = u[1 + k] * inv
    flux = [u[1 + k], u[1] * along, u[2] * along, u[3] * along, (u[4] + pressure) * along, u[5] * along]
    flux[1 + k] = flux[1 + k] + pressure
    return flux, jnp.abs(along) + jnp.sqrt(GAMMA * pressure * inv)


def face(a, b):
    (ua, fa, sa), (ub, fb, sb) = a, b
    top = jnp.maximum(sa, sb)
    return [0.5 * (fa[c] + fb[c]) - 0.5 * top * (ub[c] - ua[c]) for c in range(6)]


def pack_faces(ref, faces):
    planes, rows, lanes = ref.shape[1:]
    plane_id = lax.broadcasted_iota(jnp.int32, (planes, rows, lanes), 0)
    lane_id = lax.broadcasted_iota(jnp.int32, (planes, rows, lanes), 2)
    here = plane_id == lane_id
    for c in range(6):
        faces[0, 0, c] = ref[c, 0]
        faces[0, 1, c] = ref[c, planes - 1]
        faces[1, 0, c] = ref[c, :, 0, :]
        faces[1, 1, c] = ref[c, :, rows - 1, :]
        whole = ref[c]
        for side, lane in ((0, 0), (1, lanes - 1)):
            column = jnp.broadcast_to(whole[:, :, lane : lane + 1], (planes, rows, lanes))
            column = jnp.where(here | ((plane_id == 0) & (lane_id >= planes)), column, 0.0)
            faces[2, side, c] = jnp.sum(column, axis=0)


def tendency(u, faces, ghosts):
    shape = u[0].shape
    planes, rows, lanes = shape
    row_id = lax.broadcasted_iota(jnp.int32, shape, 1)
    lane_id = lax.broadcasted_iota(jnp.int32, shape, 2)
    result = [None] * 6

    def edge_faces(k):
        own = [[faces[k, side, c] for c in range(6)] for side in range(2)]
        out = [[ghosts[k, side, c] for c in range(6)] for side in range(2)]
        state = lambda v: (v,) + directional(v, k)
        return face(state(out[0]), state(own[0])), face(state(own[1]), state(out[1]))

    for k in range(3):
        low, high = edge_faces(k)
        flux, speed = directional(u, k)
        if k == 0:
            a = ([v[:-1] for v in u], [v[:-1] for v in flux], speed[:-1])
            b = ([v[1:] for v in u], [v[1:] for v in flux], speed[1:])
            inner = face(a, b)
            for c in range(6):
                h = jnp.concatenate([low[c][None], inner[c], high[c][None]], axis=0)
                result[c] = h[:-1] - h[1:]
            continue
        axis, length = k, shape[k]
        place = row_id if k == 1 else lane_id
        ahead = lambda v: pltpu.roll(v, length - 1, axis)
        inner = face((u, flux, speed), ([ahead(v) for v in u], [ahead(v) for v in flux], ahead(speed)))
        for c in range(6):
            if k == 1:
                lo = jnp.broadcast_to(low[c][:, None, :], shape)
                hi = jnp.broadcast_to(high[c][:, None, :], shape)
            else:
                lo = jnp.stack([jnp.broadcast_to(low[c][:, x : x + 1], (rows, lanes)) for x in range(planes)])
                hi = jnp.stack([jnp.broadcast_to(high[c][:, x : x + 1], (rows, lanes)) for x in range(planes)])
            upper = jnp.where(place == length - 1, hi, inner[c])
            lower = jnp.where(place == 0, lo, pltpu.roll(inner[c], 1, axis))
            result[c] = result[c] + (lower - upper)
    burned = RATE * u[5] * jnp.exp(-ACTIVATION * u[0] / pressure_of(u))
    result[4] = result[4] + HEAT * burned
    result[5] = result[5] - burned
    return result


def parcel_update(drop, gas):
    inv = 1.0 / gas[0]
    gas_velocity = [gas[1] * inv, gas[2] * inv, gas[3] * inv]
    gas_temp = pressure_of(gas) * inv
    vapour = gas[5] * inv
    mass, temp = drop[3], drop[4]
    root = jnp.sqrt(mass)
    inv_root = 1.0 / root
    new_mass = mass * jnp.exp(-TIME_STEP * EVAP_RATE * gas_temp * inv_root / (1.0 + vapour * vapour))
    drag = jnp.exp((-TIME_STEP / DRAG_RELAX_TIME) * inv_root)
    warm = jnp.exp((-TIME_STEP / HEATING_RELAX) * inv_root)
    new_velocity = [gas_velocity[d] + (drop[d] - gas_velocity[d]) * drag for d in range(3)]
    new_temp = gas_temp + (temp - gas_temp) * warm
    lost = mass - new_mass
    momentum = [mass * drop[d] - new_mass * new_velocity[d] for d in range(3)]
    before = drop[0] * drop[0] + drop[1] * drop[1] + drop[2] * drop[2]
    after = new_velocity[0] * new_velocity[0] + new_velocity[1] * new_velocity[1] + new_velocity[2] * new_velocity[2]
    energy = 0.5 * (mass * before - new_mass * after) + LIQUID_HEAT * (mass * temp - new_mass * new_temp)
    return new_velocity + [new_mass, new_temp], [lost] + momentum + [energy]


def split_three(v):
    head = v.astype(BF16)
    rest = v - head.astype(F32)
    middle = rest.astype(BF16)
    return head, middle, (rest - middle.astype(F32)).astype(BF16)


def kernel(
    sizes, counts_h, order_h, gas_h, parcels_h, cells_h,
    gas_out, moved,
    counts_v, order_v, gas, parcels, cells, fetch,
    faces, ghosts, stepped, hot, high_hot, sources, live, spread,
    choice, blocks, own_blocks, going, coming, arrived, count_out, count_in,
    face_send, face_recv, move_send, move_recv, count_send, count_recv,
):
    place = [lax.axis_index(a) for a in AXES]
    planes, rows, lanes = gas.shape[1:]
    slots = parcels.shape[1]
    cap = slots // 4
    group = 8
    chunks = slots // group
    half = planes // 2
    wide = half * rows

    inputs = ((gas_h, gas), (counts_h, counts_v), (order_h, order_v), (cells_h, cells), (parcels_h, parcels))
    fetches = [pltpu.make_async_copy(src, dst, fetch.at[i]) for i, (src, dst) in enumerate(inputs)]
    for copy in fetches:
        copy.start()

    def has(k, side):
        return place[k] > 0 if side == 0 else place[k] < sizes[k] - 1

    def neighbour(k, side):
        return {AXES[k]: lax.rem(place[k] + (sizes[k] - 1 if side == 0 else 1), sizes[k])}

    def copy_to(k, side, src, dst, send, recv):
        return pltpu.make_async_remote_copy(
            src_ref=src, dst_ref=dst, send_sem=send, recv_sem=recv,
            device_id=neighbour(k, side), device_id_type=MESH,
        )

    def face_copy(turn, k, side):
        return copy_to(
            k, side, faces.at[turn, k, side], ghosts.at[turn, k, 1 - side],
            face_send.at[turn, k, side], face_recv.at[turn, k, 1 - side],
        )

    def count_copy(side):
        return copy_to(0, side, count_out.at[side], count_in.at[1 - side], count_send.at[side], count_recv.at[1 - side])

    def move_copy(side):
        return copy_to(0, side, going.at[side], coming.at[1 - side], move_send.at[side], move_recv.at[1 - side])

    links = [(k, side) for k in range(3) for side in range(2) if sizes[k] > 1]

    barrier = pltpu.get_barrier_semaphore()
    arrivals = 0
    for k, side in links:
        @pl.when(has(k, side))
        def _():
            pl.semaphore_signal(barrier, inc=1, device_id=neighbour(k, side), device_id_type=MESH)
        arrivals = arrivals + has(k, side).astype(jnp.int32)

    for copy in fetches[:4]:
        copy.wait()
    kept, forward, backward = [counts_v[0:1, i : i + 1] for i in range(3)]
    u = [gas[c] for c in range(6)]
    pack_faces(gas, faces.at[0])
    count_out[0] = jnp.broadcast_to(backward, count_out.shape[1:])
    count_out[1] = jnp.broadcast_to(forward, count_out.shape[1:])
    for side in range(2):
        @pl.when(jnp.logical_not(has(0, side)))
        def _():
            count_in[side] = jnp.zeros(count_in.shape[1:], jnp.int32)
            coming[side] = jnp.zeros(coming.shape[1:], F32)

    pl.semaphore_wait(barrier, arrivals)

    def send_faces(turn):
        for k in range(3):
            for side in range(2):
                if (k, side) in links:
                    @pl.when(has(k, side))
                    def _():
                        face_copy(turn, k, side).start()

                @pl.when(jnp.logical_not(has(k, side)))
                def _():
                    ghosts[turn, k, side] = faces[turn, k, side]

    def receive_faces(turn):
        for k, side in links:
            @pl.when(has(k, side))
            def _():
                face_copy(turn, k, 1 - side).wait_recv()

    send_faces(0)
    for side in range(2):
        if sizes[0] > 1:
            @pl.when(has(0, side))
            def _():
                count_copy(side).start()

    def build(i, carry):
        cell = cells[pl.ds(i * group, group), :]
        column = (cell % lanes) + (cell // (lanes * wide)) * lanes
        high = (cell // lanes) % wide
        column = column.astype(F32).T
        column_id = lax.broadcasted_iota(jnp.int32, (lanes, 2 * lanes), 1).astype(F32)
        row_id = lax.broadcasted_iota(jnp.int32, (wide, lanes), 0)
        for j in range(group):
            here = slice(j * lanes, (j + 1) * lanes)
            match = jnp.broadcast_to(column[:, j : j + 1], column_id.shape) == column_id
            hot[pl.ds(pl.multiple_of((i * group + j) * lanes, lanes), lanes), :] = jnp.where(match, 1.0, 0.0).astype(BF16)
            high_hot[i, :, here] = jnp.where(row_id == high[j : j + 1, :], 1.0, 0.0).astype(BF16)
        return carry

    lax.fori_loop(0, chunks // 2, build, 0)
    receive_faces(0)
    change = tendency(u, faces.at[0], ghosts.at[0])
    one = [u[c] + TIME_STEP * change[c] for c in range(6)]
    for c in range(6):
        stepped[c] = one[c]
    pack_faces(stepped, faces.at[1])
    send_faces(1)

    lax.fori_loop(chunks // 2, chunks, build, 0)
    fetches[4].wait()
    slot_id = lax.broadcasted_iota(jnp.int32, (slots, slots), 0)
    turn_id = lax.broadcasted_iota(jnp.int32, (slots, slots), 1)
    used = (order_v[...] == slot_id) & (turn_id < kept + forward + backward)
    used = jnp.sum(jnp.where(used, 1.0, 0.0), axis=1, keepdims=True)
    live[...] = jnp.broadcast_to(used, live.shape)

    rows_out = slots + 2 * cap
    take_id = lax.broadcasted_iota(jnp.int32, (rows_out, slots), 0)
    from_id = lax.broadcasted_iota(jnp.int32, (rows_out, slots), 1)
    spot = jnp.where(take_id < slots, take_id, take_id - slots + kept)
    spot = jnp.where(take_id < slots + cap, spot, take_id - slots - cap + kept + forward)
    origin = jnp.where(from_id == spot, order_v[...].astype(F32), 0.0)
    origin = jnp.sum(origin, axis=1, keepdims=True)
    wide_id = lax.broadcasted_iota(jnp.int32, choice.shape, 1) % slots
    take_id = lax.broadcasted_iota(jnp.int32, choice.shape, 0)
    chosen = (wide_id.astype(F32) == origin) & ((take_id < kept) | (take_id >= slots))
    choice[...] = jnp.where(chosen, 1.0, 0.0).astype(BF16)

    receive_faces(1)
    one = [stepped[c] for c in range(6)]
    change = tendency(one, faces.at[1], ghosts.at[1])
    for c in range(6):
        v = 0.5 * gas[c] + 0.5 * (one[c] + TIME_STEP * change[c])
        stepped[c] = v

    def gather(i, carry):
        block = pl.ds(i * group, group)
        cell = cells[block, :]
        lane, high = cell % lanes, cell // lanes
        got = [jnp.zeros((group, lanes), F32)] * 6
        for x in range(planes):
            for y in range(rows):
                match = high == x * rows + y
                for c in range(6):
                    row = jnp.broadcast_to(stepped[c, x, y : y + 1, :], (group, lanes))
                    value = jnp.take_along_axis(row, lane, axis=1, mode="promise_in_bounds")
                    got[c] = jnp.where(match, value, got[c])
        new, source = parcel_update([parcels[d, block, :] for d in range(5)], got)
        for d in range(5):
            for part, term in enumerate(split_three(new[d])):
                blocks[d, pl.ds(part * slots + i * group, group), :] = term.astype(F32)
        for c in range(5):
            sources[i, c] = source[c] * live[block, :]
        return carry

    lax.fori_loop(0, chunks, gather, 0)

    for d in range(5):
        sorted_blocks = jnp.dot(choice[...], blocks[d].astype(BF16), preferred_element_type=F32)
        own_blocks[d] = sorted_blocks[:slots]
        going[1, d] = sorted_blocks[slots : slots + cap]
        going[0, d] = sorted_blocks[slots + cap :]
    for side in range(2):
        if sizes[0] > 1:
            @pl.when(has(0, side))
            def _():
                move_copy(side).start()

    def scatter(i, carry):
        source = [sources[i, c] for c in range(5)]
        head = [v.astype(BF16).astype(F32) for v in source]
        rest = [v - h for v, h in zip(source, head)]
        for j in range(group):
            here = pl.ds(pl.multiple_of((i * group + j) * lanes, lanes), lanes)
            match = high_hot[i, :, j * lanes : (j + 1) * lanes]
            for c, v in enumerate(head + rest):
                term = jnp.broadcast_to(v[j : j + 1, :], (wide, lanes)).astype(BF16)
                spread[c * wide : (c + 1) * wide, here] = match * term
        return carry

    lax.fori_loop(0, chunks, scatter, 0)
    total = jnp.dot(spread[...], hot[...], preferred_element_type=F32)
    for c in range(6):
        s = 0 if c == 5 else c
        summed = total[s * wide : (s + 1) * wide, :] + total[(5 + s) * wide : (6 + s) * wide, :]
        for part in range(2):
            part_sum = summed[:, part * lanes : (part + 1) * lanes].reshape(half, rows, lanes)
            here = slice(part * half, (part + 1) * half)
            gas_out[c, here] = stepped[c, here] + part_sum

    for side in range(2):
        if sizes[0] > 1:
            @pl.when(has(0, side))
            def _():
                count_copy(1 - side).wait_recv()
                move_copy(1 - side).wait_recv()

    place_shape = (slots, 6 * cap)
    slot_id = lax.broadcasted_iota(jnp.int32, place_shape, 0)
    block_id = lax.broadcasted_iota(jnp.int32, place_shape, 1) % (2 * cap)
    lower = jnp.broadcast_to(count_in[0, 0:1, : 6 * cap], place_shape)
    upper = jnp.broadcast_to(count_in[1, 0:1, : 6 * cap], place_shape)
    from_lower = (slot_id - kept == block_id) & (block_id < cap) & (block_id < lower)
    above = block_id - cap
    from_upper = (slot_id - kept - lower == above) & (above >= 0) & (above < upper)
    fill = jnp.where(from_lower | from_upper, 1.0, 0.0).astype(BF16)
    for d in range(5):
        for side in range(2):
            for part, term in enumerate(split_three(coming[side, d])):
                start = part * 2 * cap + side * cap
                arrived[d, start : start + cap, :] = term
        moved[d] = own_blocks[d] + jnp.dot(fill, arrived[d], preferred_element_type=F32)

    for turn in range(2):
        for k, side in links:
            @pl.when(has(k, side))
            def _():
                face_copy(turn, k, side).wait_send()
    for side in range(2):
        if sizes[0] > 1:
            @pl.when(has(0, side))
            def _():
                count_copy(side).wait_send()
                move_copy(side).wait_send()


def write_out(gas_in, moved_in, gas_out, moved_out, done):
    copies = [pltpu.make_async_copy(gas_in, gas_out, done.at[0]), pltpu.make_async_copy(moved_in, moved_out, done.at[1])]
    for copy in copies:
        copy.start()
    for copy in copies:
        copy.wait()


def body(sizes, gas, parcels, home_cell_index, order, counts):
    planes, rows, lanes = gas.shape[1:]
    parcels = jnp.transpose(parcels, (1, 0, 2))
    slots = parcels.shape[1]
    group = 8
    chunks = slots // group
    wide = planes // 2 * rows
    cap = slots // 4
    vmem = pl.BlockSpec(memory_space=pltpu.VMEM)
    hbm = pl.BlockSpec(memory_space=pltpu.HBM)
    dma = pltpu.SemaphoreType.DMA
    gas_out, moved = pl.pallas_call(
        functools.partial(kernel, sizes),
        out_shape=(
            jax.ShapeDtypeStruct(gas.shape, F32),
            jax.ShapeDtypeStruct(parcels.shape, F32),
        ),
        in_specs=[hbm] * 5,
        out_specs=(vmem, vmem),
        scratch_shapes=[
            pltpu.VMEM(counts.shape, jnp.int32),
            pltpu.VMEM(order.shape, jnp.int32),
            pltpu.VMEM(gas.shape, F32),
            pltpu.VMEM(parcels.shape, F32),
            pltpu.VMEM(home_cell_index.shape, jnp.int32),
            dma((5,)),
            pltpu.VMEM((2, 3, 2, 6, rows, lanes), F32),
            pltpu.VMEM((2, 3, 2, 6, rows, lanes), F32),
            pltpu.VMEM(gas.shape, F32),
            pltpu.VMEM((slots * lanes, 2 * lanes), BF16),
            pltpu.VMEM((chunks, wide, group * lanes), BF16),
            pltpu.VMEM((chunks, 5, group, lanes), F32),
            pltpu.VMEM((slots, lanes), F32),
            pltpu.VMEM((10 * wide, slots * lanes), BF16),
            pltpu.VMEM((slots + 2 * cap, 3 * slots), BF16),
            pltpu.VMEM((5, 3 * slots, lanes), F32),
            pltpu.VMEM(parcels.shape, F32),
            pltpu.VMEM((2, 5, cap, lanes), F32),
            pltpu.VMEM((2, 5, cap, lanes), F32),
            pltpu.VMEM((5, 6 * cap, lanes), BF16),
            pltpu.VMEM((2, 8, lanes), jnp.int32),
            pltpu.VMEM((2, 8, lanes), jnp.int32),
            dma((2, 3, 2)), dma((2, 3, 2)), dma((2,)), dma((2,)), dma((2,)), dma((2,)),
        ],
        compiler_params=pltpu.CompilerParams(
            collective_id=0, has_side_effects=True, vmem_limit_bytes=48 * 1024 * 1024
        ),
    )(*[pltpu.with_memory_space_constraint(v, pltpu.HBM) for v in (counts, order, gas, parcels, home_cell_index)])
    gas_out, moved = pl.pallas_call(
        write_out,
        out_shape=(
            jax.ShapeDtypeStruct(gas.shape, F32),
            jax.ShapeDtypeStruct(parcels.shape, F32),
        ),
        in_specs=[vmem, vmem],
        out_specs=(hbm, hbm),
        scratch_shapes=[dma((2,))],
    )(gas_out, moved)
    return gas_out, jnp.transpose(moved, (1, 0, 2))


def solution(mesh):
    in_specs = (
        P(None, "gx", "gy", "gz"),
        P(("gx", "gy", "gz"), None, None),
        P(("gx", "gy", "gz"), None),
        P(("gx", "gy", "gz"), None),
        P(("gx", "gy", "gz"), None),
    )
    out_specs = (P(None, "gx", "gy", "gz"), P(("gx", "gy", "gz"), None, None))
    sizes = tuple(mesh.shape[a] for a in AXES)
    return jax.shard_map(
        functools.partial(body, sizes), mesh=mesh, in_specs=in_specs, out_specs=out_specs, check_vma=False
    )
```

```python
import functools

import jax
import jax.numpy as jnp
from jax import lax
from jax.experimental import pallas as pl
from jax.experimental.pallas import tpu as pltpu
from jax.sharding import PartitionSpec as P

GAMMA = 1.4
TIME_STEP = 0.1
RATE = 3.0
ACTIVATION = 2.0
HEAT = 5.0
DRAG_RELAX_TIME = 0.4
HEATING_RELAX = 0.6
EVAP_RATE = 1.5
LIQUID_HEAT = 2.0
AXES = ("gx", "gy", "gz")
MESH = pl.DeviceIdType.MESH
F32 = jnp.float32
BF16 = jnp.bfloat16


def pressure_of(u):
    motion_energy = u[1] * u[1] + u[2] * u[2] + u[3] * u[3]
    return (GAMMA - 1.0) * (u[4] - 0.5 * motion_energy / u[0])


def base_of(u):
    inv = 1.0 / u[0]
    pressure = (GAMMA - 1.0) * (u[4] - 0.5 * inv * (u[1] * u[1] + u[2] * u[2] + u[3] * u[3]))
    return inv, pressure, jnp.sqrt(GAMMA * pressure * inv)


def directional(u, base, k):
    inv, pressure, sound = base
    along = u[1 + k] * inv
    flux = [u[1 + k], u[1] * along, u[2] * along, u[3] * along, (u[4] + pressure) * along, u[5] * along]
    flux[1 + k] = flux[1 + k] + pressure
    return flux, jnp.abs(along) + sound


def face(a, b):
    (ua, fa, sa), (ub, fb, sb) = a, b
    top = jnp.maximum(sa, sb)
    return [0.5 * ((fa[c] + fb[c]) - top * (ub[c] - ua[c])) for c in range(6)]


def pack_faces(ref, faces):
    planes, rows, lanes = ref.shape[1:]
    plane_id = lax.broadcasted_iota(jnp.int32, (planes, rows, lanes), 0)
    lane_id = lax.broadcasted_iota(jnp.int32, (planes, rows, lanes), 2)
    here = plane_id == lane_id
    for c in range(6):
        faces[0, 0, c] = ref[c, 0]
        faces[0, 1, c] = ref[c, planes - 1]
        faces[1, 0, c] = ref[c, :, 0, :]
        faces[1, 1, c] = ref[c, :, rows - 1, :]
        whole = ref[c]
        for side, lane in ((0, 0), (1, lanes - 1)):
            column = jnp.broadcast_to(whole[:, :, lane : lane + 1], (planes, rows, lanes))
            column = jnp.where(here | ((plane_id == 0) & (lane_id >= planes)), column, 0.0)
            faces[2, side, c] = jnp.sum(column, axis=0)


def inner_change(ref, change):
    planes, rows, lanes = ref.shape[1:]
    place_ids = [lax.broadcasted_iota(jnp.int32, (rows, lanes), d) for d in range(2)]
    before, behind = None, None
    for x in range(planes):
        u = [ref[c, x] for c in range(6)]
        base = base_of(u)
        now = (u,) + directional(u, base, 0)
        burned = RATE * u[5] * jnp.exp(-ACTIVATION * u[0] / base[1])
        result = [None] * 4 + [HEAT * burned, -burned]
        for k in (1, 2):
            flux, speed = directional(u, base, k)
            length = (rows, lanes)[k - 1]
            ahead = lambda v: pltpu.roll(v, length - 1, k - 1)
            upper = face((u, flux, speed), ([ahead(v) for v in u], [ahead(v) for v in flux], ahead(speed)))
            for c in range(6):
                h = jnp.where(place_ids[k - 1] == length - 1, 0.0, upper[c])
                d = pltpu.roll(h, 1, k - 1) - h
                result[c] = d if result[c] is None else result[c] + d
        if x > 0:
            between = face(before, now)
            for c in range(6):
                change[c, x - 1] = behind[c] - between[c]
                result[c] = result[c] + between[c]
        before, behind = now, result
    for c in range(6):
        change[c, planes - 1] = behind[c]


def edge_states(faces, states):
    for k in range(3):
        for side in range(2):
            u = [faces[k, side, c] for c in range(6)]
            flux, speed = directional(u, base_of(u), k)
            for c in range(6):
                states[k, side, c] = flux[c]
            states[k, side, 6] = speed


def full_change(change, faces, states, ghosts):
    shape = change.shape[1:]
    planes, rows, lanes = shape
    row_id = lax.broadcasted_iota(jnp.int32, shape, 1)
    lane_id = lax.broadcasted_iota(jnp.int32, shape, 2)
    edges = []
    for k in range(3):
        own, out = [], []
        for side in range(2):
            u = [ghosts[k, side, c] for c in range(6)]
            out.append((u,) + directional(u, base_of(u), k))
            own.append(([faces[k, side, c] for c in range(6)], [states[k, side, c] for c in range(6)], states[k, side, 6]))
        edges.append((face(out[0], own[0]), face(own[1], out[1])))
    result = []
    for c in range(6):
        low, high = edges[1][0][c], edges[1][1][c]
        low, high = [jnp.broadcast_to(v[:, None, :], shape) for v in (low, high)]
        total = change[c] + jnp.where(row_id == 0, low, jnp.where(row_id == rows - 1, -high, 0.0))
        low, high = edges[2][0][c], edges[2][1][c]
        low, high = [
            jnp.stack([jnp.broadcast_to(v[:, x : x + 1], (rows, lanes)) for x in range(planes)]) for v in (low, high)
        ]
        total = total + jnp.where(lane_id == 0, low, jnp.where(lane_id == lanes - 1, -high, 0.0))
        low, high = edges[0][0][c], edges[0][1][c]
        first, last = total[:1] + low[None], total[-1:] - high[None]
        result.append(jnp.concatenate([first, total[1:-1], last], axis=0))
    return result


def parcel_update(drop, gas):
    inv = 1.0 / gas[0]
    gas_velocity = [gas[1] * inv, gas[2] * inv, gas[3] * inv]
    gas_temp = pressure_of(gas) * inv
    vapour = gas[5] * inv
    mass, temp = drop[3], drop[4]
    root = jnp.sqrt(mass)
    inv_root = 1.0 / root
    new_mass = mass * jnp.exp(-TIME_STEP * EVAP_RATE * gas_temp * inv_root / (1.0 + vapour * vapour))
    drag = jnp.exp((-TIME_STEP / DRAG_RELAX_TIME) * inv_root)
    warm = jnp.exp((-TIME_STEP / HEATING_RELAX) * inv_root)
    new_velocity = [gas_velocity[d] + (drop[d] - gas_velocity[d]) * drag for d in range(3)]
    new_temp = gas_temp + (temp - gas_temp) * warm
    lost = mass - new_mass
    momentum = [mass * drop[d] - new_mass * new_velocity[d] for d in range(3)]
    before = drop[0] * drop[0] + drop[1] * drop[1] + drop[2] * drop[2]
    after = new_velocity[0] * new_velocity[0] + new_velocity[1] * new_velocity[1] + new_velocity[2] * new_velocity[2]
    energy = 0.5 * (mass * before - new_mass * after) + LIQUID_HEAT * (mass * temp - new_mass * new_temp)
    return new_velocity + [new_mass, new_temp], [lost] + momentum + [energy]


def split_three(v):
    head = v.astype(BF16)
    rest = v - head.astype(F32)
    middle = rest.astype(BF16)
    return head, middle, (rest - middle.astype(F32)).astype(BF16)


def kernel(
    sizes, counts_h, order_h, gas_h, parcels_h, cells_h,
    gas_out, moved,
    counts_v, order_v, gas, parcels, cells, fetch,
    faces, ghosts, states, change, stepped, copies, hot, high_hot, sources, live, spread,
    choice, blocks, own_blocks, going, coming, arrived, count_out, count_in,
    face_send, face_recv, move_send, move_recv, count_send, count_recv,
):
    place = [lax.axis_index(a) for a in AXES]
    planes, rows, lanes = gas.shape[1:]
    slots = parcels.shape[1]
    cap = slots // 4
    group = 8
    chunks = slots // group
    half = planes // 2
    wide = half * rows

    inputs = ((gas_h, gas), (counts_h, counts_v), (order_h, order_v), (cells_h, cells), (parcels_h, parcels))
    fetches = [pltpu.make_async_copy(src, dst, fetch.at[i]) for i, (src, dst) in enumerate(inputs)]
    for copy in fetches:
        copy.start()

    def has(k, side):
        return place[k] > 0 if side == 0 else place[k] < sizes[k] - 1

    def neighbour(k, side):
        return {AXES[k]: lax.rem(place[k] + (sizes[k] - 1 if side == 0 else 1), sizes[k])}

    def copy_to(k, side, src, dst, send, recv):
        return pltpu.make_async_remote_copy(
            src_ref=src, dst_ref=dst, send_sem=send, recv_sem=recv,
            device_id=neighbour(k, side), device_id_type=MESH,
        )

    def face_copy(turn, k, side):
        return copy_to(
            k, side, faces.at[turn, k, side], ghosts.at[turn, k, 1 - side],
            face_send.at[turn, k, side], face_recv.at[turn, k, 1 - side],
        )

    def count_copy(side):
        return copy_to(0, side, count_out.at[side], count_in.at[1 - side], count_send.at[side], count_recv.at[1 - side])

    def move_copy(side):
        return copy_to(0, side, going.at[side], coming.at[1 - side], move_send.at[side], move_recv.at[1 - side])

    links = [(k, side) for k in range(3) for side in range(2) if sizes[k] > 1]

    barrier = pltpu.get_barrier_semaphore()
    arrivals = 0
    for k, side in links:
        @pl.when(has(k, side))
        def _():
            pl.semaphore_signal(barrier, inc=1, device_id=neighbour(k, side), device_id_type=MESH)
        arrivals = arrivals + has(k, side).astype(jnp.int32)

    for copy in fetches[:4]:
        copy.wait()
    kept, forward, backward = [counts_v[0:1, i : i + 1] for i in range(3)]
    pack_faces(gas, faces.at[0])
    count_out[0] = jnp.broadcast_to(backward, count_out.shape[1:])
    count_out[1] = jnp.broadcast_to(forward, count_out.shape[1:])
    for side in range(2):
        @pl.when(jnp.logical_not(has(0, side)))
        def _():
            count_in[side] = jnp.zeros(count_in.shape[1:], jnp.int32)
            coming[side] = jnp.zeros(coming.shape[1:], F32)

    pl.semaphore_wait(barrier, arrivals)

    def send_faces(turn):
        for k in range(3):
            for side in range(2):
                if (k, side) in links:
                    @pl.when(has(k, side))
                    def _():
                        face_copy(turn, k, side).start()

                @pl.when(jnp.logical_not(has(k, side)))
                def _():
                    ghosts[turn, k, side] = faces[turn, k, side]

    def receive_faces(turn):
        for k, side in links:
            @pl.when(has(k, side))
            def _():
                face_copy(turn, k, 1 - side).wait_recv()

    send_faces(0)
    for side in range(2):
        if sizes[0] > 1:
            @pl.when(has(0, side))
            def _():
                count_copy(side).start()

    def build(i, carry):
        cell = cells[pl.ds(i * group, group), :]
        column = (cell % lanes) + (cell // (lanes * wide)) * lanes
        high = (cell // lanes) % wide
        column = column.astype(F32).T
        column_id = lax.broadcasted_iota(jnp.int32, (lanes, 2 * lanes), 1).astype(F32)
        row_id = lax.broadcasted_iota(jnp.int32, (wide, lanes), 0)
        for j in range(group):
            here = slice(j * lanes, (j + 1) * lanes)
            match = jnp.broadcast_to(column[:, j : j + 1], column_id.shape) == column_id
            hot[pl.ds(pl.multiple_of((i * group + j) * lanes, lanes), lanes), :] = jnp.where(match, 1.0, 0.0).astype(BF16)
            high_hot[i, :, here] = jnp.where(row_id == high[j : j + 1, :], 1.0, 0.0).astype(BF16)
        return carry

    inner_change(gas, change)
    edge_states(faces.at[0], states)
    lax.fori_loop(0, chunks // 2, build, 0)
    receive_faces(0)
    both = full_change(change, faces.at[0], states, ghosts.at[0])
    for c in range(6):
        stepped[c] = gas[c] + TIME_STEP * both[c]
    pack_faces(stepped, faces.at[1])
    send_faces(1)
    inner_change(stepped, change)
    edge_states(faces.at[1], states)

    lax.fori_loop(chunks // 2, chunks, build, 0)
    fetches[4].wait()
    slot_id = lax.broadcasted_iota(jnp.int32, (slots, slots), 0)
    turn_id = lax.broadcasted_iota(jnp.int32, (slots, slots), 1)
    used = (order_v[...] == slot_id) & (turn_id < kept + forward + backward)
    used = jnp.sum(jnp.where(used, 1.0, 0.0), axis=1, keepdims=True)
    live[...] = jnp.broadcast_to(used, live.shape)

    rows_out = slots + 2 * cap
    take_id = lax.broadcasted_iota(jnp.int32, (rows_out, slots), 0)
    from_id = lax.broadcasted_iota(jnp.int32, (rows_out, slots), 1)
    spot = jnp.where(take_id < slots, take_id, take_id - slots + kept)
    spot = jnp.where(take_id < slots + cap, spot, take_id - slots - cap + kept + forward)
    origin = jnp.where(from_id == spot, order_v[...].astype(F32), 0.0)
    origin = jnp.sum(origin, axis=1, keepdims=True)
    wide_id = lax.broadcasted_iota(jnp.int32, choice.shape, 1) % slots
    take_id = lax.broadcasted_iota(jnp.int32, choice.shape, 0)
    chosen = (wide_id.astype(F32) == origin) & ((take_id < kept) | (take_id >= slots))
    choice[...] = jnp.where(chosen, 1.0, 0.0).astype(BF16)

    receive_faces(1)
    both = full_change(change, faces.at[1], states, ghosts.at[1])
    for c in range(6):
        v = 0.5 * gas[c] + 0.5 * (stepped[c] + TIME_STEP * both[c])
        stepped[c] = v
        for x in range(planes):
            for y in range(rows):
                copies[x, y, c] = jnp.broadcast_to(v[x, y : y + 1, :], (group, lanes))

    def spread_out(i):
        source = [sources[i, c] for c in range(5)]
        head = [v.astype(BF16).astype(F32) for v in source]
        rest = [v - h for v, h in zip(source, head)]
        for j in range(group):
            here = pl.ds(pl.multiple_of((i * group + j) * lanes, lanes), lanes)
            match = high_hot[i, :, j * lanes : (j + 1) * lanes]
            for c, v in enumerate(head + rest):
                term = jnp.broadcast_to(v[j : j + 1, :], (wide, lanes)).astype(BF16)
                spread[c * wide : (c + 1) * wide, here] = match * term

    for c in range(5):
        sources[0, c] = jnp.zeros((group, lanes), F32)

    def gather(i, carry):
        spread_out(jnp.maximum(i - 1, 0))
        block = pl.ds(i * group, group)
        cell = cells[block, :]
        lane, high = cell % lanes, cell // lanes
        got = [jnp.zeros((group, lanes), F32)] * 6
        for x in range(planes):
            for y in range(rows):
                match = high == x * rows + y
                for c in range(6):
                    value = jnp.take_along_axis(copies[x, y, c], lane, axis=1, mode="promise_in_bounds")
                    got[c] = jnp.where(match, value, got[c])
        new, source = parcel_update([parcels[d, block, :] for d in range(5)], got)
        for d in range(5):
            for part, term in enumerate(split_three(new[d])):
                blocks[d, pl.ds(part * slots + i * group, group), :] = term.astype(F32)
        for c in range(5):
            sources[i, c] = source[c] * live[block, :]
        return carry

    lax.fori_loop(0, chunks, gather, 0)

    for d in range(5):
        sorted_blocks = jnp.dot(choice[...], blocks[d].astype(BF16), preferred_element_type=F32)
        own_blocks[d] = sorted_blocks[:slots]
        going[1, d] = sorted_blocks[slots : slots + cap]
        going[0, d] = sorted_blocks[slots + cap :]
    for side in range(2):
        if sizes[0] > 1:
            @pl.when(has(0, side))
            def _():
                move_copy(side).start()

    spread_out(chunks - 1)
    total = jnp.dot(spread[...], hot[...], preferred_element_type=F32)
    for c in range(6):
        s = 0 if c == 5 else c
        summed = total[s * wide : (s + 1) * wide, :] + total[(5 + s) * wide : (6 + s) * wide, :]
        for part in range(2):
            part_sum = summed[:, part * lanes : (part + 1) * lanes].reshape(half, rows, lanes)
            here = slice(part * half, (part + 1) * half)
            gas_out[c, here] = stepped[c, here] + part_sum

    for side in range(2):
        if sizes[0] > 1:
            @pl.when(has(0, side))
            def _():
                count_copy(1 - side).wait_recv()
                move_copy(1 - side).wait_recv()

    place_shape = (slots, 6 * cap)
    slot_id = lax.broadcasted_iota(jnp.int32, place_shape, 0)
    block_id = lax.broadcasted_iota(jnp.int32, place_shape, 1) % (2 * cap)
    lower = jnp.broadcast_to(count_in[0, 0:1, : 6 * cap], place_shape)
    upper = jnp.broadcast_to(count_in[1, 0:1, : 6 * cap], place_shape)
    from_lower = (slot_id - kept == block_id) & (block_id < cap) & (block_id < lower)
    above = block_id - cap
    from_upper = (slot_id - kept - lower == above) & (above >= 0) & (above < upper)
    fill = jnp.where(from_lower | from_upper, 1.0, 0.0).astype(BF16)
    for d in range(5):
        for side in range(2):
            for part, term in enumerate(split_three(coming[side, d])):
                start = part * 2 * cap + side * cap
                arrived[d, start : start + cap, :] = term
        moved[d] = own_blocks[d] + jnp.dot(fill, arrived[d], preferred_element_type=F32)

    for turn in range(2):
        for k, side in links:
            @pl.when(has(k, side))
            def _():
                face_copy(turn, k, side).wait_send()
    for side in range(2):
        if sizes[0] > 1:
            @pl.when(has(0, side))
            def _():
                count_copy(side).wait_send()
                move_copy(side).wait_send()


def body(sizes, gas, parcels, home_cell_index, order, counts):
    planes, rows, lanes = gas.shape[1:]
    parcels = jnp.transpose(parcels, (1, 0, 2))
    slots = parcels.shape[1]
    group = 8
    chunks = slots // group
    wide = planes // 2 * rows
    cap = slots // 4
    vmem = pl.BlockSpec(memory_space=pltpu.VMEM)
    hbm = pl.BlockSpec(memory_space=pltpu.HBM)
    dma = pltpu.SemaphoreType.DMA
    gas_out, moved = pl.pallas_call(
        functools.partial(kernel, sizes),
        out_shape=(pltpu.VMEM(gas.shape, F32), pltpu.VMEM(parcels.shape, F32)),
        in_specs=[hbm] * 5,
        out_specs=(vmem, vmem),
        scratch_shapes=[
            pltpu.VMEM(counts.shape, jnp.int32),
            pltpu.VMEM(order.shape, jnp.int32),
            pltpu.VMEM(gas.shape, F32),
            pltpu.VMEM(parcels.shape, F32),
            pltpu.VMEM(home_cell_index.shape, jnp.int32),
            dma((5,)),
            pltpu.VMEM((2, 3, 2, 6, rows, lanes), F32),
            pltpu.VMEM((2, 3, 2, 6, rows, lanes), F32),
            pltpu.VMEM((3, 2, 7, rows, lanes), F32),
            pltpu.VMEM(gas.shape, F32),
            pltpu.VMEM(gas.shape, F32),
            pltpu.VMEM((planes, rows, 6, group, lanes), F32),
            pltpu.VMEM((slots * lanes, 2 * lanes), BF16),
            pltpu.VMEM((chunks, wide, group * lanes), BF16),
            pltpu.VMEM((chunks, 5, group, lanes), F32),
            pltpu.VMEM((slots, lanes), F32),
            pltpu.VMEM((10 * wide, slots * lanes), BF16),
            pltpu.VMEM((slots + 2 * cap, 3 * slots), BF16),
            pltpu.VMEM((5, 3 * slots, lanes), F32),
            pltpu.VMEM(parcels.shape, F32),
            pltpu.VMEM((2, 5, cap, lanes), F32),
            pltpu.VMEM((2, 5, cap, lanes), F32),
            pltpu.VMEM((5, 6 * cap, lanes), BF16),
            pltpu.VMEM((2, 8, lanes), jnp.int32),
            pltpu.VMEM((2, 8, lanes), jnp.int32),
            dma((2, 3, 2)), dma((2, 3, 2)), dma((2,)), dma((2,)), dma((2,)), dma((2,)),
        ],
        compiler_params=pltpu.CompilerParams(
            collective_id=0, has_side_effects=True, vmem_limit_bytes=48 * 1024 * 1024
        ),
    )(*[pltpu.with_memory_space_constraint(v, pltpu.HBM) for v in (counts, order, gas, parcels, home_cell_index)])
    return gas_out, jnp.transpose(moved, (1, 0, 2))


def solution(mesh):
    in_specs = (
        P(None, "gx", "gy", "gz"),
        P(("gx", "gy", "gz"), None, None),
        P(("gx", "gy", "gz"), None),
        P(("gx", "gy", "gz"), None),
        P(("gx", "gy", "gz"), None),
    )
    out_specs = (P(None, "gx", "gy", "gz"), P(("gx", "gy", "gz"), None, None))
    sizes = tuple(mesh.shape[a] for a in AXES)
    return jax.shard_map(
        functools.partial(body, sizes), mesh=mesh, in_specs=in_specs, out_specs=out_specs, check_vma=False
    )
```

```python
import functools

import jax
import jax.numpy as jnp
from jax import lax
from jax.experimental import pallas as pl
from jax.experimental.pallas import tpu as pltpu
from jax.sharding import PartitionSpec as P

GAMMA = 1.4
TIME_STEP = 0.1
RATE = 3.0
ACTIVATION = 2.0
HEAT = 5.0
DRAG_RELAX_TIME = 0.4
HEATING_RELAX = 0.6
EVAP_RATE = 1.5
LIQUID_HEAT = 2.0
AXES = ("gx", "gy", "gz")
MESH = pl.DeviceIdType.MESH
F32 = jnp.float32
BF16 = jnp.bfloat16


def pressure_of(u):
    motion_energy = u[1] * u[1] + u[2] * u[2] + u[3] * u[3]
    return (GAMMA - 1.0) * (u[4] - 0.5 * motion_energy / u[0])


def base_of(u):
    inv = 1.0 / u[0]
    pressure = (GAMMA - 1.0) * (u[4] - 0.5 * inv * (u[1] * u[1] + u[2] * u[2] + u[3] * u[3]))
    return inv, pressure, jnp.sqrt(GAMMA * pressure * inv)


def directional(u, base, k):
    inv, pressure, sound = base
    along = u[1 + k] * inv
    flux = [u[1 + k], u[1] * along, u[2] * along, u[3] * along, (u[4] + pressure) * along, u[5] * along]
    flux[1 + k] = flux[1 + k] + pressure
    return flux, jnp.abs(along) + sound


def face(a, b):
    (ua, fa, sa), (ub, fb, sb) = a, b
    top = jnp.maximum(sa, sb)
    return [0.5 * ((fa[c] + fb[c]) - top * (ub[c] - ua[c])) for c in range(6)]


def pack_faces(ref, faces):
    planes, rows, lanes = ref.shape[1:]
    plane_id = lax.broadcasted_iota(jnp.int32, (planes, rows, lanes), 0)
    lane_id = lax.broadcasted_iota(jnp.int32, (planes, rows, lanes), 2)
    here = plane_id == lane_id
    for c in range(6):
        faces[0, 0, c] = ref[c, 0]
        faces[0, 1, c] = ref[c, planes - 1]
        faces[1, 0, c] = ref[c, :, 0, :]
        faces[1, 1, c] = ref[c, :, rows - 1, :]
        whole = ref[c]
        for side, lane in ((0, 0), (1, lanes - 1)):
            column = jnp.broadcast_to(whole[:, :, lane : lane + 1], (planes, rows, lanes))
            column = jnp.where(here | ((plane_id == 0) & (lane_id >= planes)), column, 0.0)
            faces[2, side, c] = jnp.sum(column, axis=0)


def inner_change(ref, change):
    planes, rows, lanes = ref.shape[1:]
    place_ids = [lax.broadcasted_iota(jnp.int32, (rows, lanes), d) for d in range(2)]
    before, behind = None, None
    for x in range(planes):
        u = [ref[c, x] for c in range(6)]
        base = base_of(u)
        now = (u,) + directional(u, base, 0)
        burned = RATE * u[5] * jnp.exp(-ACTIVATION * u[0] / base[1])
        result = [None] * 4 + [HEAT * burned, -burned]
        for k in (1, 2):
            flux, speed = directional(u, base, k)
            length = (rows, lanes)[k - 1]
            ahead = lambda v: pltpu.roll(v, length - 1, k - 1)
            upper = face((u, flux, speed), ([ahead(v) for v in u], [ahead(v) for v in flux], ahead(speed)))
            for c in range(6):
                h = jnp.where(place_ids[k - 1] == length - 1, 0.0, upper[c])
                d = pltpu.roll(h, 1, k - 1) - h
                result[c] = d if result[c] is None else result[c] + d
        if x > 0:
            between = face(before, now)
            for c in range(6):
                change[c, x - 1] = behind[c] - between[c]
                result[c] = result[c] + between[c]
        before, behind = now, result
    for c in range(6):
        change[c, planes - 1] = behind[c]


def edge_states(faces, states):
    for k in range(3):
        for side in range(2):
            u = [faces[k, side, c] for c in range(6)]
            flux, speed = directional(u, base_of(u), k)
            for c in range(6):
                states[k, side, c] = flux[c]
            states[k, side, 6] = speed


def full_change(change, faces, states, ghosts):
    shape = change.shape[1:]
    planes, rows, lanes = shape
    row_id = lax.broadcasted_iota(jnp.int32, shape, 1)
    lane_id = lax.broadcasted_iota(jnp.int32, shape, 2)
    edges = []
    for k in range(3):
        own, out = [], []
        for side in range(2):
            u = [ghosts[k, side, c] for c in range(6)]
            out.append((u,) + directional(u, base_of(u), k))
            own.append(([faces[k, side, c] for c in range(6)], [states[k, side, c] for c in range(6)], states[k, side, 6]))
        edges.append((face(out[0], own[0]), face(own[1], out[1])))
    result = []
    for c in range(6):
        low, high = edges[1][0][c], edges[1][1][c]
        low, high = [jnp.broadcast_to(v[:, None, :], shape) for v in (low, high)]
        total = change[c] + jnp.where(row_id == 0, low, jnp.where(row_id == rows - 1, -high, 0.0))
        low, high = edges[2][0][c], edges[2][1][c]
        low, high = [
            jnp.stack([jnp.broadcast_to(v[:, x : x + 1], (rows, lanes)) for x in range(planes)]) for v in (low, high)
        ]
        total = total + jnp.where(lane_id == 0, low, jnp.where(lane_id == lanes - 1, -high, 0.0))
        low, high = edges[0][0][c], edges[0][1][c]
        first, last = total[:1] + low[None], total[-1:] - high[None]
        result.append(jnp.concatenate([first, total[1:-1], last], axis=0))
    return result


def parcel_update(drop, gas):
    inv = 1.0 / gas[0]
    gas_velocity = [gas[1] * inv, gas[2] * inv, gas[3] * inv]
    gas_temp = pressure_of(gas) * inv
    vapour = gas[5] * inv
    mass, temp = drop[3], drop[4]
    root = jnp.sqrt(mass)
    inv_root = 1.0 / root
    new_mass = mass * jnp.exp(-TIME_STEP * EVAP_RATE * gas_temp * inv_root / (1.0 + vapour * vapour))
    drag = jnp.exp((-TIME_STEP / DRAG_RELAX_TIME) * inv_root)
    warm = jnp.exp((-TIME_STEP / HEATING_RELAX) * inv_root)
    new_velocity = [gas_velocity[d] + (drop[d] - gas_velocity[d]) * drag for d in range(3)]
    new_temp = gas_temp + (temp - gas_temp) * warm
    lost = mass - new_mass
    momentum = [mass * drop[d] - new_mass * new_velocity[d] for d in range(3)]
    before = drop[0] * drop[0] + drop[1] * drop[1] + drop[2] * drop[2]
    after = new_velocity[0] * new_velocity[0] + new_velocity[1] * new_velocity[1] + new_velocity[2] * new_velocity[2]
    energy = 0.5 * (mass * before - new_mass * after) + LIQUID_HEAT * (mass * temp - new_mass * new_temp)
    return new_velocity + [new_mass, new_temp], [lost] + momentum + [energy]


def split_three(v):
    head = v.astype(BF16)
    rest = v - head.astype(F32)
    middle = rest.astype(BF16)
    return head, middle, (rest - middle.astype(F32)).astype(BF16)


def kernel(
    sizes, counts_h, order_h, gas_h, parcels_h, cells_h,
    gas_out, moved,
    counts_v, order_v, gas, parcels, cells, fetch,
    faces, ghosts, states, change, stepped, table, carried, hot, high_hot, sources, live, spread,
    choice, blocks, own_blocks, going, coming, arrived, count_out, count_in,
    face_send, face_recv, move_send, move_recv, count_send, count_recv,
):
    place = [lax.axis_index(a) for a in AXES]
    planes, rows, lanes = gas.shape[1:]
    slots = parcels.shape[1]
    cap = slots // 4
    group = 8
    chunks = slots // group
    half = planes // 2
    wide = half * rows

    inputs = ((gas_h, gas), (counts_h, counts_v), (order_h, order_v), (cells_h, cells), (parcels_h, parcels))
    fetches = [pltpu.make_async_copy(src, dst, fetch.at[i]) for i, (src, dst) in enumerate(inputs)]
    for copy in fetches:
        copy.start()

    def has(k, side):
        return place[k] > 0 if side == 0 else place[k] < sizes[k] - 1

    def neighbour(k, side):
        return {AXES[k]: lax.rem(place[k] + (sizes[k] - 1 if side == 0 else 1), sizes[k])}

    def copy_to(k, side, src, dst, send, recv):
        return pltpu.make_async_remote_copy(
            src_ref=src, dst_ref=dst, send_sem=send, recv_sem=recv,
            device_id=neighbour(k, side), device_id_type=MESH,
        )

    def face_copy(turn, k, side):
        return copy_to(
            k, side, faces.at[turn, k, side], ghosts.at[turn, k, 1 - side],
            face_send.at[turn, k, side], face_recv.at[turn, k, 1 - side],
        )

    def count_copy(side):
        return copy_to(0, side, count_out.at[side], count_in.at[1 - side], count_send.at[side], count_recv.at[1 - side])

    def move_copy(side):
        return copy_to(0, side, going.at[side], coming.at[1 - side], move_send.at[side], move_recv.at[1 - side])

    links = [(k, side) for k in range(3) for side in range(2) if sizes[k] > 1]

    barrier = pltpu.get_barrier_semaphore()
    arrivals = 0
    for k, side in links:
        @pl.when(has(k, side))
        def _():
            pl.semaphore_signal(barrier, inc=1, device_id=neighbour(k, side), device_id_type=MESH)
        arrivals = arrivals + has(k, side).astype(jnp.int32)

    for copy in fetches[:4]:
        copy.wait()
    kept, forward, backward = [counts_v[0:1, i : i + 1] for i in range(3)]
    pack_faces(gas, faces.at[0])
    count_out[0] = jnp.broadcast_to(backward, count_out.shape[1:])
    count_out[1] = jnp.broadcast_to(forward, count_out.shape[1:])
    for side in range(2):
        @pl.when(jnp.logical_not(has(0, side)))
        def _():
            count_in[side] = jnp.zeros(count_in.shape[1:], jnp.int32)
            coming[side] = jnp.zeros(coming.shape[1:], F32)

    pl.semaphore_wait(barrier, arrivals)

    def send_faces(turn):
        for k in range(3):
            for side in range(2):
                if (k, side) in links:
                    @pl.when(has(k, side))
                    def _():
                        face_copy(turn, k, side).start()

                @pl.when(jnp.logical_not(has(k, side)))
                def _():
                    ghosts[turn, k, side] = faces[turn, k, side]

    def receive_faces(turn):
        for k, side in links:
            @pl.when(has(k, side))
            def _():
                face_copy(turn, k, 1 - side).wait_recv()

    send_faces(0)
    for side in range(2):
        if sizes[0] > 1:
            @pl.when(has(0, side))
            def _():
                count_copy(side).start()

    def build(i, carry):
        cell = cells[pl.ds(i * group, group), :]
        column = ((cell % lanes) + (cell // (lanes * wide)) * lanes).astype(F32)
        high = ((cell // lanes) % wide).astype(F32)
        column_id = lax.broadcasted_iota(jnp.int32, (2 * lanes, lanes), 0).astype(F32).astype(BF16)
        row_id = lax.broadcasted_iota(jnp.int32, (wide, lanes), 0).astype(F32).astype(BF16)
        one, none = jnp.ones((), BF16), jnp.zeros((), BF16)
        for j in range(group):
            here = pl.ds(pl.multiple_of((i * group + j) * lanes, lanes), lanes)
            match = jnp.broadcast_to(column[j : j + 1, :], column_id.shape).astype(BF16) == column_id
            hot[:, here] = jnp.where(match, one, none)
            match = jnp.broadcast_to(high[j : j + 1, :], row_id.shape).astype(BF16) == row_id
            high_hot[:, here] = jnp.where(match, one, none)
        return carry

    inner_change(gas, change)
    edge_states(faces.at[0], states)
    lax.fori_loop(0, chunks // 2, build, 0)
    receive_faces(0)
    both = full_change(change, faces.at[0], states, ghosts.at[0])
    for c in range(6):
        stepped[c] = gas[c] + TIME_STEP * both[c]
    pack_faces(stepped, faces.at[1])
    send_faces(1)
    inner_change(stepped, change)
    edge_states(faces.at[1], states)

    lax.fori_loop(chunks // 2, chunks, build, 0)
    fetches[4].wait()
    slot_id = lax.broadcasted_iota(jnp.int32, (slots, slots), 0)
    turn_id = lax.broadcasted_iota(jnp.int32, (slots, slots), 1)
    used = (order_v[...] == slot_id) & (turn_id < kept + forward + backward)
    used = jnp.sum(jnp.where(used, 1.0, 0.0), axis=1, keepdims=True)
    live[...] = jnp.broadcast_to(used, live.shape)

    rows_out = slots + 2 * cap
    take_id = lax.broadcasted_iota(jnp.int32, (rows_out, slots), 0)
    from_id = lax.broadcasted_iota(jnp.int32, (rows_out, slots), 1)
    spot = jnp.where(take_id < slots, take_id, take_id - slots + kept)
    spot = jnp.where(take_id < slots + cap, spot, take_id - slots - cap + kept + forward)
    origin = jnp.where(from_id == spot, order_v[...].astype(F32), 0.0)
    origin = jnp.sum(origin, axis=1, keepdims=True)
    wide_id = lax.broadcasted_iota(jnp.int32, choice.shape, 1) % slots
    take_id = lax.broadcasted_iota(jnp.int32, choice.shape, 0)
    chosen = (wide_id.astype(F32) == origin) & ((take_id < kept) | (take_id >= slots))
    choice[...] = jnp.where(chosen, 1.0, 0.0).astype(BF16)

    receive_faces(1)
    both = full_change(change, faces.at[1], states, ghosts.at[1])
    for c in range(6):
        v = 0.5 * gas[c] + 0.5 * (stepped[c] + TIME_STEP * both[c])
        stepped[c] = v
        for part in range(2):
            terms = split_three(v[part * half : (part + 1) * half].reshape(wide, lanes))
            for t in range(2):
                start = (6 * t + c) * wide
                table[start : start + wide, part * lanes : (part + 1) * lanes] = terms[t]

    def spread_out(i, carry):
        source = [sources[i, c] for c in range(5)]
        head = [v.astype(BF16).astype(F32) for v in source]
        rest = [v - h for v, h in zip(source, head)]
        for j in range(group):
            here = pl.ds(pl.multiple_of((i * group + j) * lanes, lanes), lanes)
            match = high_hot[:, here]
            for c, v in enumerate(head + rest):
                term = jnp.broadcast_to(v[j : j + 1, :], (wide, lanes)).astype(BF16)
                spread[c * wide : (c + 1) * wide, here] = match * term
        return carry

    def gather(i, carry):
        for n in range(2):
            gather_chunk(2 * i + n)
        return carry

    def gather_chunk(i):
        block = pl.ds(pl.multiple_of(i * group, group), group)
        cell = cells[block, :]
        high = (cell // lanes) % wide
        row_id = lax.broadcasted_iota(jnp.int32, (wide, lanes), 0)
        every = pl.ds(pl.multiple_of(i * group * lanes, group * lanes), group * lanes)
        found = jnp.dot(table[...], hot[:, every], preferred_element_type=F32)
        for j in range(group):
            here = slice(j * lanes, (j + 1) * lanes)
            match = row_id == high[j : j + 1, :]
            for c in range(6):
                v = found[c * wide : (c + 1) * wide, here] + found[(6 + c) * wide : (7 + c) * wide, here]
                carried[i, c, j : j + 1, :] = jnp.sum(jnp.where(match, v, 0.0), axis=0, keepdims=True)
        got = [carried[i, c] for c in range(6)]
        new, source = parcel_update([parcels[d, block, :] for d in range(5)], got)
        for d in range(5):
            for part, term in enumerate(split_three(new[d])):
                blocks[d, pl.ds(pl.multiple_of(part * slots + i * group, group), group), :] = term.astype(F32)
        for c in range(5):
            sources[i, c] = source[c] * live[block, :]

    lax.fori_loop(0, chunks // 2, gather, 0)

    for d in range(5):
        sorted_blocks = jnp.dot(choice[...], blocks[d].astype(BF16), preferred_element_type=F32)
        own_blocks[d] = sorted_blocks[:slots]
        going[1, d] = sorted_blocks[slots : slots + cap]
        going[0, d] = sorted_blocks[slots + cap :]
    for side in range(2):
        if sizes[0] > 1:
            @pl.when(has(0, side))
            def _():
                move_copy(side).start()

    lax.fori_loop(0, chunks, spread_out, 0)
    total = lax.dot_general(spread[...], hot[...], (((1,), (1,)), ((), ())), preferred_element_type=F32)
    for c in range(6):
        s = 0 if c == 5 else c
        summed = total[s * wide : (s + 1) * wide, :] + total[(5 + s) * wide : (6 + s) * wide, :]
        for part in range(2):
            part_sum = summed[:, part * lanes : (part + 1) * lanes].reshape(half, rows, lanes)
            here = slice(part * half, (part + 1) * half)
            gas_out[c, here] = stepped[c, here] + part_sum

    for side in range(2):
        if sizes[0] > 1:
            @pl.when(has(0, side))
            def _():
                count_copy(1 - side).wait_recv()
                move_copy(1 - side).wait_recv()

    place_shape = (slots, 6 * cap)
    slot_id = lax.broadcasted_iota(jnp.int32, place_shape, 0)
    block_id = lax.broadcasted_iota(jnp.int32, place_shape, 1) % (2 * cap)
    lower = jnp.broadcast_to(count_in[0, 0:1, : 6 * cap], place_shape)
    upper = jnp.broadcast_to(count_in[1, 0:1, : 6 * cap], place_shape)
    from_lower = (slot_id - kept == block_id) & (block_id < cap) & (block_id < lower)
    above = block_id - cap
    from_upper = (slot_id - kept - lower == above) & (above >= 0) & (above < upper)
    fill = jnp.where(from_lower | from_upper, 1.0, 0.0).astype(BF16)
    for d in range(5):
        for side in range(2):
            for part, term in enumerate(split_three(coming[side, d])):
                start = part * 2 * cap + side * cap
                arrived[d, start : start + cap, :] = term
        moved[d] = own_blocks[d] + jnp.dot(fill, arrived[d], preferred_element_type=F32)

    for turn in range(2):
        for k, side in links:
            @pl.when(has(k, side))
            def _():
                face_copy(turn, k, side).wait_send()
    for side in range(2):
        if sizes[0] > 1:
            @pl.when(has(0, side))
            def _():
                count_copy(side).wait_send()
                move_copy(side).wait_send()


def body(sizes, gas, parcels, home_cell_index, order, counts):
    planes, rows, lanes = gas.shape[1:]
    parcels = jnp.transpose(parcels, (1, 0, 2))
    slots = parcels.shape[1]
    group = 8
    chunks = slots // group
    wide = planes // 2 * rows
    cap = slots // 4
    vmem = pl.BlockSpec(memory_space=pltpu.VMEM)
    hbm = pl.BlockSpec(memory_space=pltpu.HBM)
    dma = pltpu.SemaphoreType.DMA
    gas_out, moved = pl.pallas_call(
        functools.partial(kernel, sizes),
        out_shape=(pltpu.VMEM(gas.shape, F32), pltpu.VMEM(parcels.shape, F32)),
        in_specs=[hbm] * 5,
        out_specs=(vmem, vmem),
        scratch_shapes=[
            pltpu.VMEM(counts.shape, jnp.int32),
            pltpu.VMEM(order.shape, jnp.int32),
            pltpu.VMEM(gas.shape, F32),
            pltpu.VMEM(parcels.shape, F32),
            pltpu.VMEM(home_cell_index.shape, jnp.int32),
            dma((5,)),
            pltpu.VMEM((2, 3, 2, 6, rows, lanes), F32),
            pltpu.VMEM((2, 3, 2, 6, rows, lanes), F32),
            pltpu.VMEM((3, 2, 7, rows, lanes), F32),
            pltpu.VMEM(gas.shape, F32),
            pltpu.VMEM(gas.shape, F32),
            pltpu.VMEM((12 * wide, 2 * lanes), BF16),
            pltpu.VMEM((chunks, 6, group, lanes), F32),
            pltpu.VMEM((2 * lanes, slots * lanes), BF16),
            pltpu.VMEM((wide, slots * lanes), BF16),
            pltpu.VMEM((chunks, 5, group, lanes), F32),
            pltpu.VMEM((slots, lanes), F32),
            pltpu.VMEM((10 * wide, slots * lanes), BF16),
            pltpu.VMEM((slots + 2 * cap, 3 * slots), BF16),
            pltpu.VMEM((5, 3 * slots, lanes), F32),
            pltpu.VMEM(parcels.shape, F32),
            pltpu.VMEM((2, 5, cap, lanes), F32),
            pltpu.VMEM((2, 5, cap, lanes), F32),
            pltpu.VMEM((5, 6 * cap, lanes), BF16),
            pltpu.VMEM((2, 8, lanes), jnp.int32),
            pltpu.VMEM((2, 8, lanes), jnp.int32),
            dma((2, 3, 2)), dma((2, 3, 2)), dma((2,)), dma((2,)), dma((2,)), dma((2,)),
        ],
        compiler_params=pltpu.CompilerParams(
            collective_id=0, has_side_effects=True, vmem_limit_bytes=48 * 1024 * 1024
        ),
    )(*[pltpu.with_memory_space_constraint(v, pltpu.HBM) for v in (counts, order, gas, parcels, home_cell_index)])
    return gas_out, jnp.transpose(moved, (1, 0, 2))


def solution(mesh):
    in_specs = (
        P(None, "gx", "gy", "gz"),
        P(("gx", "gy", "gz"), None, None),
        P(("gx", "gy", "gz"), None),
        P(("gx", "gy", "gz"), None),
        P(("gx", "gy", "gz"), None),
    )
    out_specs = (P(None, "gx", "gy", "gz"), P(("gx", "gy", "gz"), None, None))
    sizes = tuple(mesh.shape[a] for a in AXES)
    return jax.shard_map(
        functools.partial(body, sizes), mesh=mesh, in_specs=in_specs, out_specs=out_specs, check_vma=False
    )
```

```python
import functools

import jax
import jax.numpy as jnp
from jax import lax
from jax.experimental import pallas as pl
from jax.experimental.pallas import tpu as pltpu
from jax.sharding import PartitionSpec as P

GAMMA = 1.4
TIME_STEP = 0.1
RATE = 3.0
ACTIVATION = 2.0
HEAT = 5.0
DRAG_RELAX_TIME = 0.4
HEATING_RELAX = 0.6
EVAP_RATE = 1.5
LIQUID_HEAT = 2.0
AXES = ("gx", "gy", "gz")
MESH = pl.DeviceIdType.MESH
F32 = jnp.float32
BF16 = jnp.bfloat16
QUARTERS = 4


def pressure_of(u):
    motion_energy = u[1] * u[1] + u[2] * u[2] + u[3] * u[3]
    return (GAMMA - 1.0) * (u[4] - 0.5 * motion_energy / u[0])


def base_of(u):
    inv = 1.0 / u[0]
    pressure = (GAMMA - 1.0) * (u[4] - 0.5 * inv * (u[1] * u[1] + u[2] * u[2] + u[3] * u[3]))
    return inv, pressure, jnp.sqrt(GAMMA * pressure * inv)


def directional(u, base, k):
    inv, pressure, sound = base
    along = u[1 + k] * inv
    flux = [u[1 + k], u[1] * along, u[2] * along, u[3] * along, (u[4] + pressure) * along, u[5] * along]
    flux[1 + k] = flux[1 + k] + pressure
    return flux, jnp.abs(along) + sound


def face(a, b):
    (ua, fa, sa), (ub, fb, sb) = a, b
    top = jnp.maximum(sa, sb)
    return [0.5 * ((fa[c] + fb[c]) - top * (ub[c] - ua[c])) for c in range(6)]


def pack_faces(ref, faces):
    planes, rows, lanes = ref.shape[1:]
    plane_id = lax.broadcasted_iota(jnp.int32, (planes, rows, lanes), 0)
    lane_id = lax.broadcasted_iota(jnp.int32, (planes, rows, lanes), 2)
    here = plane_id == lane_id
    for c in range(6):
        faces[0, 0, c] = ref[c, 0]
        faces[0, 1, c] = ref[c, planes - 1]
        faces[1, 0, c] = ref[c, :, 0, :]
        faces[1, 1, c] = ref[c, :, rows - 1, :]
        whole = ref[c]
        for side, lane in ((0, 0), (1, lanes - 1)):
            column = jnp.broadcast_to(whole[:, :, lane : lane + 1], (planes, rows, lanes))
            column = jnp.where(here | ((plane_id == 0) & (lane_id >= planes)), column, 0.0)
            faces[2, side, c] = jnp.sum(column, axis=0)


def inner_change(ref, change):
    planes, rows, lanes = ref.shape[1:]
    place_ids = [lax.broadcasted_iota(jnp.int32, (rows, lanes), d) for d in range(2)]
    before, behind = None, None
    for x in range(planes):
        u = [ref[c, x] for c in range(6)]
        base = base_of(u)
        now = (u,) + directional(u, base, 0)
        burned = RATE * u[5] * jnp.exp(-ACTIVATION * u[0] / base[1])
        result = [None] * 4 + [HEAT * burned, -burned]
        for k in (1, 2):
            flux, speed = directional(u, base, k)
            length = (rows, lanes)[k - 1]
            ahead = lambda v: pltpu.roll(v, length - 1, k - 1)
            upper = face((u, flux, speed), ([ahead(v) for v in u], [ahead(v) for v in flux], ahead(speed)))
            for c in range(6):
                h = jnp.where(place_ids[k - 1] == length - 1, 0.0, upper[c])
                d = pltpu.roll(h, 1, k - 1) - h
                result[c] = d if result[c] is None else result[c] + d
        if x > 0:
            between = face(before, now)
            for c in range(6):
                change[c, x - 1] = behind[c] - between[c]
                result[c] = result[c] + between[c]
        before, behind = now, result
    for c in range(6):
        change[c, planes - 1] = behind[c]


def edge_states(faces, states):
    for k in range(3):
        for side in range(2):
            u = [faces[k, side, c] for c in range(6)]
            flux, speed = directional(u, base_of(u), k)
            for c in range(6):
                states[k, side, c] = flux[c]
            states[k, side, 6] = speed


def full_change(change, faces, states, ghosts):
    shape = change.shape[1:]
    planes, rows, lanes = shape
    row_id = lax.broadcasted_iota(jnp.int32, shape, 1)
    lane_id = lax.broadcasted_iota(jnp.int32, shape, 2)
    edges = []
    for k in range(3):
        own, out = [], []
        for side in range(2):
            u = [ghosts[k, side, c] for c in range(6)]
            out.append((u,) + directional(u, base_of(u), k))
            own.append(([faces[k, side, c] for c in range(6)], [states[k, side, c] for c in range(6)], states[k, side, 6]))
        edges.append((face(out[0], own[0]), face(own[1], out[1])))
    result = []
    for c in range(6):
        low, high = edges[1][0][c], edges[1][1][c]
        low, high = [jnp.broadcast_to(v[:, None, :], shape) for v in (low, high)]
        total = change[c] + jnp.where(row_id == 0, low, jnp.where(row_id == rows - 1, -high, 0.0))
        low, high = edges[2][0][c], edges[2][1][c]
        low, high = [
            jnp.stack([jnp.broadcast_to(v[:, x : x + 1], (rows, lanes)) for x in range(planes)]) for v in (low, high)
        ]
        total = total + jnp.where(lane_id == 0, low, jnp.where(lane_id == lanes - 1, -high, 0.0))
        low, high = edges[0][0][c], edges[0][1][c]
        first, last = total[:1] + low[None], total[-1:] - high[None]
        result.append(jnp.concatenate([first, total[1:-1], last], axis=0))
    return result


def parcel_update(drop, gas):
    inv = 1.0 / gas[0]
    gas_velocity = [gas[1] * inv, gas[2] * inv, gas[3] * inv]
    gas_temp = pressure_of(gas) * inv
    vapour = gas[5] * inv
    mass, temp = drop[3], drop[4]
    root = jnp.sqrt(mass)
    inv_root = 1.0 / root
    new_mass = mass * jnp.exp(-TIME_STEP * EVAP_RATE * gas_temp * inv_root / (1.0 + vapour * vapour))
    drag = jnp.exp((-TIME_STEP / DRAG_RELAX_TIME) * inv_root)
    warm = jnp.exp((-TIME_STEP / HEATING_RELAX) * inv_root)
    new_velocity = [gas_velocity[d] + (drop[d] - gas_velocity[d]) * drag for d in range(3)]
    new_temp = gas_temp + (temp - gas_temp) * warm
    lost = mass - new_mass
    momentum = [mass * drop[d] - new_mass * new_velocity[d] for d in range(3)]
    before = drop[0] * drop[0] + drop[1] * drop[1] + drop[2] * drop[2]
    after = new_velocity[0] * new_velocity[0] + new_velocity[1] * new_velocity[1] + new_velocity[2] * new_velocity[2]
    energy = 0.5 * (mass * before - new_mass * after) + LIQUID_HEAT * (mass * temp - new_mass * new_temp)
    return new_velocity + [new_mass, new_temp], [lost] + momentum + [energy]


def row_sums(parts):
    count = len(parts)
    row_id = lax.broadcasted_iota(jnp.int32, parts[0].shape, 0)
    step = 1
    while step < count:
        low = (row_id // step) % 2 == 0
        parts = [
            jnp.where(low, a, b) + pltpu.roll(jnp.where(low, b, a), step, 0) for a, b in zip(parts[::2], parts[1::2])
        ]
        step *= 2
    return parts[0]


def split_three(v):
    head = v.astype(BF16)
    rest = v - head.astype(F32)
    middle = rest.astype(BF16)
    return head, middle, (rest - middle.astype(F32)).astype(BF16)


def kernel(
    sizes, counts_h, order_h, gas_h, parcels_h, cells_h,
    gas_out, moved,
    counts_v, order_v, gas, parcels, cells, fetch,
    faces, ghosts, states, change, stepped, table, hot, high_hot, sources, live, *rest,
):
    spreads, rest = rest[:QUARTERS], rest[QUARTERS:]
    choice, blocks, own_blocks, going, coming, arrived, count_out, count_in = rest[:8]
    face_send, face_recv, move_send, move_recv, count_send, count_recv = rest[8:]
    place = [lax.axis_index(a) for a in AXES]
    planes, rows, lanes = gas.shape[1:]
    slots = parcels.shape[1]
    cap = slots // 4
    group = 8
    chunks = slots // group
    half = planes // 2
    wide = half * rows

    inputs = ((gas_h, gas), (counts_h, counts_v), (order_h, order_v), (cells_h, cells), (parcels_h, parcels))
    fetches = [pltpu.make_async_copy(src, dst, fetch.at[i]) for i, (src, dst) in enumerate(inputs)]
    for copy in fetches:
        copy.start()

    def has(k, side):
        return place[k] > 0 if side == 0 else place[k] < sizes[k] - 1

    def neighbour(k, side):
        return {AXES[k]: lax.rem(place[k] + (sizes[k] - 1 if side == 0 else 1), sizes[k])}

    def copy_to(k, side, src, dst, send, recv):
        return pltpu.make_async_remote_copy(
            src_ref=src, dst_ref=dst, send_sem=send, recv_sem=recv,
            device_id=neighbour(k, side), device_id_type=MESH,
        )

    def face_copy(turn, k, side):
        return copy_to(
            k, side, faces.at[turn, k, side], ghosts.at[turn, k, 1 - side],
            face_send.at[turn, k, side], face_recv.at[turn, k, 1 - side],
        )

    def count_copy(side):
        return copy_to(0, side, count_out.at[side], count_in.at[1 - side], count_send.at[side], count_recv.at[1 - side])

    def move_copy(side):
        return copy_to(0, side, going.at[side], coming.at[1 - side], move_send.at[side], move_recv.at[1 - side])

    links = [(k, side) for k in range(3) for side in range(2) if sizes[k] > 1]

    barrier = pltpu.get_barrier_semaphore()
    arrivals = 0
    for k, side in links:
        @pl.when(has(k, side))
        def _():
            pl.semaphore_signal(barrier, inc=1, device_id=neighbour(k, side), device_id_type=MESH)
        arrivals = arrivals + has(k, side).astype(jnp.int32)

    for copy in fetches[:4]:
        copy.wait()
    kept, forward, backward = [counts_v[0:1, i : i + 1] for i in range(3)]
    pack_faces(gas, faces.at[0])
    count_out[0] = jnp.broadcast_to(backward, count_out.shape[1:])
    count_out[1] = jnp.broadcast_to(forward, count_out.shape[1:])
    for side in range(2):
        @pl.when(jnp.logical_not(has(0, side)))
        def _():
            count_in[side] = jnp.zeros(count_in.shape[1:], jnp.int32)
            coming[side] = jnp.zeros(coming.shape[1:], F32)

    pl.semaphore_wait(barrier, arrivals)

    def send_faces(turn):
        for k in range(3):
            for side in range(2):
                if (k, side) in links:
                    @pl.when(has(k, side))
                    def _():
                        face_copy(turn, k, side).start()

                @pl.when(jnp.logical_not(has(k, side)))
                def _():
                    ghosts[turn, k, side] = faces[turn, k, side]

    def receive_faces(turn):
        for k, side in links:
            @pl.when(has(k, side))
            def _():
                face_copy(turn, k, 1 - side).wait_recv()

    send_faces(0)
    for side in range(2):
        if sizes[0] > 1:
            @pl.when(has(0, side))
            def _():
                count_copy(side).start()

    def build(i, carry):
        cell = cells[pl.ds(i * group, group), :]
        column = ((cell % lanes) + (cell // (lanes * wide)) * lanes).astype(F32)
        high = ((cell // lanes) % wide).astype(F32)
        column_id = lax.broadcasted_iota(jnp.int32, (2 * lanes, lanes), 0).astype(F32).astype(BF16)
        row_id = lax.broadcasted_iota(jnp.int32, (wide, lanes), 0).astype(F32).astype(BF16)
        one, none = jnp.ones((), BF16), jnp.zeros((), BF16)
        for j in range(group):
            here = pl.ds(pl.multiple_of((i * group + j) * lanes, lanes), lanes)
            match = jnp.broadcast_to(column[j : j + 1, :], column_id.shape).astype(BF16) == column_id
            hot[:, here] = jnp.where(match, one, none)
            match = jnp.broadcast_to(high[j : j + 1, :], row_id.shape).astype(BF16) == row_id
            high_hot[:, here] = jnp.where(match, one, none)
        return carry

    inner_change(gas, change)
    edge_states(faces.at[0], states)
    lax.fori_loop(0, chunks // 2, build, 0)
    receive_faces(0)
    both = full_change(change, faces.at[0], states, ghosts.at[0])
    for c in range(6):
        stepped[c] = gas[c] + TIME_STEP * both[c]
    pack_faces(stepped, faces.at[1])
    send_faces(1)
    inner_change(stepped, change)
    edge_states(faces.at[1], states)

    lax.fori_loop(chunks // 2, chunks, build, 0)
    fetches[4].wait()
    slot_id = lax.broadcasted_iota(jnp.int32, (slots, slots), 0)
    turn_id = lax.broadcasted_iota(jnp.int32, (slots, slots), 1)
    used = (order_v[...] == slot_id) & (turn_id < kept + forward + backward)
    used = jnp.sum(jnp.where(used, 1.0, 0.0), axis=1, keepdims=True)
    live[...] = jnp.broadcast_to(used, live.shape)

    rows_out = slots + 2 * cap
    take_id = lax.broadcasted_iota(jnp.int32, (rows_out, slots), 0)
    from_id = lax.broadcasted_iota(jnp.int32, (rows_out, slots), 1)
    spot = jnp.where(take_id < slots, take_id, take_id - slots + kept)
    spot = jnp.where(take_id < slots + cap, spot, take_id - slots - cap + kept + forward)
    origin = jnp.where(from_id == spot, order_v[...].astype(F32), 0.0)
    origin = jnp.sum(origin, axis=1, keepdims=True)
    wide_id = lax.broadcasted_iota(jnp.int32, choice.shape, 1) % slots
    take_id = lax.broadcasted_iota(jnp.int32, choice.shape, 0)
    chosen = (wide_id.astype(F32) == origin) & ((take_id < kept) | (take_id >= slots))
    choice[...] = jnp.where(chosen, 1.0, 0.0).astype(BF16)

    receive_faces(1)
    both = full_change(change, faces.at[1], states, ghosts.at[1])
    for c in range(6):
        v = 0.5 * gas[c] + 0.5 * (stepped[c] + TIME_STEP * both[c])
        stepped[c] = v
        for part in range(2):
            terms = split_three(v[part * half : (part + 1) * half].reshape(wide, lanes))
            for t in range(2):
                start = (6 * t + c) * wide
                table[start : start + wide, part * lanes : (part + 1) * lanes] = terms[t]

    def spread_out(i, spread, n):
        source = [sources[i, c] for c in range(5)]
        head = [v.astype(BF16).astype(F32) for v in source]
        rest = [v - h for v, h in zip(source, head)]
        for j in range(group):
            match = high_hot[:, (i * group + j) * lanes : (i * group + j + 1) * lanes]
            here = slice((n * group + j) * lanes, (n * group + j + 1) * lanes)
            for c, v in enumerate(head + rest):
                term = jnp.broadcast_to(v[j : j + 1, :], (wide, lanes)).astype(BF16)
                spread[c * wide : (c + 1) * wide, here] = match * term

    def gather(i, carry):
        for n in range(2):
            gather_chunk(2 * i + n)
        return carry

    def gather_chunk(i):
        block = pl.ds(pl.multiple_of(i * group, group), group)
        cell = cells[block, :]
        high = (cell // lanes) % wide
        row_id = lax.broadcasted_iota(jnp.int32, (wide, lanes), 0)
        every = pl.ds(pl.multiple_of(i * group * lanes, group * lanes), group * lanes)
        found = jnp.dot(table[...], hot[:, every], preferred_element_type=F32)
        parts = [[None] * group for _ in range(6)]
        for j in range(group):
            here = slice(j * lanes, (j + 1) * lanes)
            match = row_id == high[j : j + 1, :]
            for c in range(6):
                v = found[c * wide : (c + 1) * wide, here] + found[(6 + c) * wide : (7 + c) * wide, here]
                v = jnp.where(match, v, 0.0)
                parts[c][j] = sum(v[r : r + group] for r in range(group, wide, group)) + v[:group]
        got = [row_sums(v) for v in parts]
        new, source = parcel_update([parcels[d, block, :] for d in range(5)], got)
        for d in range(5):
            for part, term in enumerate(split_three(new[d])):
                blocks[d, pl.ds(pl.multiple_of(part * slots + i * group, group), group), :] = term.astype(F32)
        for c in range(5):
            sources[i, c] = source[c] * live[block, :]

    lax.fori_loop(0, chunks // 2, gather, 0)

    for d in range(5):
        sorted_blocks = jnp.dot(choice[...], blocks[d].astype(BF16), preferred_element_type=F32)
        own_blocks[d] = sorted_blocks[:slots]
        going[1, d] = sorted_blocks[slots : slots + cap]
        going[0, d] = sorted_blocks[slots + cap :]
    for side in range(2):
        if sizes[0] > 1:
            @pl.when(has(0, side))
            def _():
                move_copy(side).start()

    share = chunks // len(spreads)
    total = 0.0
    for q, spread in enumerate(spreads):
        for n in range(share):
            spread_out(q * share + n, spread, n)
        there = slice(q * share * group * lanes, (q + 1) * share * group * lanes)
        total = total + lax.dot_general(
            spread[...], hot[:, there], (((1,), (1,)), ((), ())), preferred_element_type=F32
        )
    for c in range(6):
        s = 0 if c == 5 else c
        summed = total[s * wide : (s + 1) * wide, :] + total[(5 + s) * wide : (6 + s) * wide, :]
        for part in range(2):
            part_sum = summed[:, part * lanes : (part + 1) * lanes].reshape(half, rows, lanes)
            here = slice(part * half, (part + 1) * half)
            gas_out[c, here] = stepped[c, here] + part_sum

    for side in range(2):
        if sizes[0] > 1:
            @pl.when(has(0, side))
            def _():
                count_copy(1 - side).wait_recv()
                move_copy(1 - side).wait_recv()

    place_shape = (slots, 6 * cap)
    slot_id = lax.broadcasted_iota(jnp.int32, place_shape, 0)
    block_id = lax.broadcasted_iota(jnp.int32, place_shape, 1) % (2 * cap)
    lower = jnp.broadcast_to(count_in[0, 0:1, : 6 * cap], place_shape)
    upper = jnp.broadcast_to(count_in[1, 0:1, : 6 * cap], place_shape)
    from_lower = (slot_id - kept == block_id) & (block_id < cap) & (block_id < lower)
    above = block_id - cap
    from_upper = (slot_id - kept - lower == above) & (above >= 0) & (above < upper)
    fill = jnp.where(from_lower | from_upper, 1.0, 0.0).astype(BF16)
    for d in range(5):
        for side in range(2):
            for part, term in enumerate(split_three(coming[side, d])):
                start = part * 2 * cap + side * cap
                arrived[d, start : start + cap, :] = term
        moved[d] = own_blocks[d] + jnp.dot(fill, arrived[d], preferred_element_type=F32)

    for turn in range(2):
        for k, side in links:
            @pl.when(has(k, side))
            def _():
                face_copy(turn, k, side).wait_send()
    for side in range(2):
        if sizes[0] > 1:
            @pl.when(has(0, side))
            def _():
                count_copy(side).wait_send()
                move_copy(side).wait_send()


def body(sizes, gas, parcels, home_cell_index, order, counts):
    planes, rows, lanes = gas.shape[1:]
    parcels = jnp.transpose(parcels, (1, 0, 2))
    slots = parcels.shape[1]
    group = 8
    chunks = slots // group
    wide = planes // 2 * rows
    cap = slots // 4
    vmem = pl.BlockSpec(memory_space=pltpu.VMEM)
    hbm = pl.BlockSpec(memory_space=pltpu.HBM)
    dma = pltpu.SemaphoreType.DMA
    gas_out, moved = pl.pallas_call(
        functools.partial(kernel, sizes),
        out_shape=(pltpu.VMEM(gas.shape, F32), pltpu.VMEM(parcels.shape, F32)),
        in_specs=[hbm] * 5,
        out_specs=(vmem, vmem),
        scratch_shapes=[
            pltpu.VMEM(counts.shape, jnp.int32),
            pltpu.VMEM(order.shape, jnp.int32),
            pltpu.VMEM(gas.shape, F32),
            pltpu.VMEM(parcels.shape, F32),
            pltpu.VMEM(home_cell_index.shape, jnp.int32),
            dma((5,)),
            pltpu.VMEM((2, 3, 2, 6, rows, lanes), F32),
            pltpu.VMEM((2, 3, 2, 6, rows, lanes), F32),
            pltpu.VMEM((3, 2, 7, rows, lanes), F32),
            pltpu.VMEM(gas.shape, F32),
            pltpu.VMEM(gas.shape, F32),
            pltpu.VMEM((12 * wide, 2 * lanes), BF16),
            pltpu.VMEM((2 * lanes, slots * lanes), BF16),
            pltpu.VMEM((wide, slots * lanes), BF16),
            pltpu.VMEM((chunks, 5, group, lanes), F32),
            pltpu.VMEM((slots, lanes), F32),
            *[pltpu.VMEM((10 * wide, slots * lanes // QUARTERS), BF16)] * QUARTERS,
            pltpu.VMEM((slots + 2 * cap, 3 * slots), BF16),
            pltpu.VMEM((5, 3 * slots, lanes), F32),
            pltpu.VMEM(parcels.shape, F32),
            pltpu.VMEM((2, 5, cap, lanes), F32),
            pltpu.VMEM((2, 5, cap, lanes), F32),
            pltpu.VMEM((5, 6 * cap, lanes), BF16),
            pltpu.VMEM((2, 8, lanes), jnp.int32),
            pltpu.VMEM((2, 8, lanes), jnp.int32),
            dma((2, 3, 2)), dma((2, 3, 2)), dma((2,)), dma((2,)), dma((2,)), dma((2,)),
        ],
        compiler_params=pltpu.CompilerParams(
            collective_id=0, has_side_effects=True, vmem_limit_bytes=48 * 1024 * 1024
        ),
    )(*[pltpu.with_memory_space_constraint(v, pltpu.HBM) for v in (counts, order, gas, parcels, home_cell_index)])
    return gas_out, jnp.transpose(moved, (1, 0, 2))


def solution(mesh):
    in_specs = (
        P(None, "gx", "gy", "gz"),
        P(("gx", "gy", "gz"), None, None),
        P(("gx", "gy", "gz"), None),
        P(("gx", "gy", "gz"), None),
        P(("gx", "gy", "gz"), None),
    )
    out_specs = (P(None, "gx", "gy", "gz"), P(("gx", "gy", "gz"), None, None))
    sizes = tuple(mesh.shape[a] for a in AXES)
    return jax.shard_map(
        functools.partial(body, sizes), mesh=mesh, in_specs=in_specs, out_specs=out_specs, check_vma=False
    )
```

```python
import functools

import jax
import jax.numpy as jnp
from jax import lax
from jax.experimental import pallas as pl
from jax.experimental.pallas import tpu as pltpu
from jax.sharding import PartitionSpec as P

GAMMA = 1.4
TIME_STEP = 0.1
RATE = 3.0
ACTIVATION = 2.0
HEAT = 5.0
DRAG_RELAX_TIME = 0.4
HEATING_RELAX = 0.6
EVAP_RATE = 1.5
LIQUID_HEAT = 2.0
AXES = ("gx", "gy", "gz")
MESH = pl.DeviceIdType.MESH
F32 = jnp.float32
BF16 = jnp.bfloat16
QUARTERS = 4


def pressure_of(u):
    motion_energy = u[1] * u[1] + u[2] * u[2] + u[3] * u[3]
    return (GAMMA - 1.0) * (u[4] - 0.5 * motion_energy / u[0])


def base_of(u):
    inv = 1.0 / u[0]
    pressure = (GAMMA - 1.0) * (u[4] - 0.5 * inv * (u[1] * u[1] + u[2] * u[2] + u[3] * u[3]))
    return inv, pressure, jnp.sqrt(GAMMA * pressure * inv)


def directional(u, base, k):
    inv, pressure, sound = base
    along = u[1 + k] * inv
    flux = [u[1 + k], u[1] * along, u[2] * along, u[3] * along, (u[4] + pressure) * along, u[5] * along]
    flux[1 + k] = flux[1 + k] + pressure
    return flux, jnp.abs(along) + sound


def face(a, b):
    (ua, fa, sa), (ub, fb, sb) = a, b
    top = jnp.maximum(sa, sb)
    return [0.5 * ((fa[c] + fb[c]) - top * (ub[c] - ua[c])) for c in range(6)]


def pack_faces(ref, faces):
    planes, rows, lanes = ref.shape[1:]
    lane_id = lax.broadcasted_iota(jnp.int32, (rows, lanes), 1)
    for c in range(6):
        faces[0, 0, c] = ref[c, 0]
        faces[0, 1, c] = ref[c, planes - 1]
        faces[1, 0, c] = ref[c, :, 0, :]
        faces[1, 1, c] = ref[c, :, rows - 1, :]
        low = high = None
        for x in range(planes):
            turned = pltpu.roll(ref[c, x], x + 1, 1)
            low = turned if low is None else jnp.where(lane_id == x + 1, turned, low)
            high = turned if high is None else jnp.where(lane_id == x, turned, high)
        faces[2, 0, c] = pltpu.roll(low, lanes - 1, 1)
        faces[2, 1, c] = high


def base_of(u):
    inv = 1.0 / u[0]
    pressure = (GAMMA - 1.0) * (u[4] - 0.5 * inv * (u[1] * u[1] + u[2] * u[2] + u[3] * u[3]))
    return inv, pressure, jnp.sqrt(GAMMA * pressure * inv)


def directional(u, base, k):
    inv, pressure, sound = base
    along = u[1 + k] * inv
    flux = [u[1 + k], u[1] * along, u[2] * along, u[3] * along, (u[4] + pressure) * along, u[5] * along]
    flux[1 + k] = flux[1 + k] + pressure
    return flux, jnp.abs(along) + sound


def face(a, b):
    (ua, fa, sa), (ub, fb, sb) = a, b
    top = jnp.maximum(sa, sb)
    return [0.5 * ((fa[c] + fb[c]) - top * (ub[c] - ua[c])) for c in range(6)]


def pack_faces(ref, faces):
    planes, rows, lanes = ref.shape[1:]
    plane_id = lax.broadcasted_iota(jnp.int32, (planes, rows, lanes), 0)
    lane_id = lax.broadcasted_iota(jnp.int32, (planes, rows, lanes), 2)
    here = plane_id == lane_id
    for c in range(6):
        faces[0, 0, c] = ref[c, 0]
        faces[0, 1, c] = ref[c, planes - 1]
        faces[1, 0, c] = ref[c, :, 0, :]
        faces[1, 1, c] = ref[c, :, rows - 1, :]
        whole = ref[c]
        for side, lane in ((0, 0), (1, lanes - 1)):
            column = jnp.broadcast_to(whole[:, :, lane : lane + 1], (planes, rows, lanes))
            column = jnp.where(here | ((plane_id == 0) & (lane_id >= planes)), column, 0.0)
            faces[2, side, c] = jnp.sum(column, axis=0)


def inner_change(ref, change):
    planes, rows, lanes = ref.shape[1:]
    place_ids = [lax.broadcasted_iota(jnp.int32, (rows, lanes), d) for d in range(2)]
    before, behind = None, None
    for x in range(planes):
        u = [ref[c, x] for c in range(6)]
        base = base_of(u)
        now = (u,) + directional(u, base, 0)
        burned = RATE * u[5] * jnp.exp(-ACTIVATION * u[0] / base[1])
        result = [None] * 4 + [HEAT * burned, -burned]
        for k in (1, 2):
            flux, speed = directional(u, base, k)
            length = (rows, lanes)[k - 1]
            ahead = lambda v: pltpu.roll(v, length - 1, k - 1)
            upper = face((u, flux, speed), ([ahead(v) for v in u], [ahead(v) for v in flux], ahead(speed)))
            for c in range(6):
                h = jnp.where(place_ids[k - 1] == length - 1, 0.0, upper[c])
                d = pltpu.roll(h, 1, k - 1) - h
                result[c] = d if result[c] is None else result[c] + d
        if x > 0:
            between = face(before, now)
            for c in range(6):
                change[c, x - 1] = behind[c] - between[c]
                result[c] = result[c] + between[c]
        before, behind = now, result
    for c in range(6):
        change[c, planes - 1] = behind[c]


def edge_states(faces, states):
    for k in range(3):
        for side in range(2):
            u = [faces[k, side, c] for c in range(6)]
            flux, speed = directional(u, base_of(u), k)
            for c in range(6):
                states[k, side, c] = flux[c]
            states[k, side, 6] = speed


def full_change(change, faces, states, ghosts):
    shape = change.shape[1:]
    planes, rows, lanes = shape
    row_id = lax.broadcasted_iota(jnp.int32, shape, 1)
    flat_id = lax.broadcasted_iota(jnp.int32, (rows, lanes), 1)
    edges = []
    for k in range(3):
        own, out = [], []
        for side in range(2):
            u = [ghosts[k, side, c] for c in range(6)]
            out.append((u,) + directional(u, base_of(u), k))
            own.append(([faces[k, side, c] for c in range(6)], [states[k, side, c] for c in range(6)], states[k, side, 6]))
        edges.append((face(out[0], own[0]), face(own[1], out[1])))
    result = []
    for c in range(6):
        low, high = edges[1][0][c], edges[1][1][c]
        low, high = [jnp.broadcast_to(v[:, None, :], shape) for v in (low, high)]
        total = change[c] + jnp.where(row_id == 0, low, jnp.where(row_id == rows - 1, -high, 0.0))
        low, high = edges[2][0][c], pltpu.roll(-edges[2][1][c], lanes - 1, 1)
        ends = []
        for x in range(planes):
            v = jnp.where(flat_id == x, low, high)
            v = pltpu.roll(v, lanes - x, 1) if x else v
            ends.append(jnp.where((flat_id == 0) | (flat_id == lanes - 1), v, 0.0))
        total = total + jnp.stack(ends)
        low, high = edges[0][0][c], edges[0][1][c]
        first, last = total[:1] + low[None], total[-1:] - high[None]
        result.append(jnp.concatenate([first, total[1:-1], last], axis=0))
    return result


def parcel_update(drop, gas):
    inv = 1.0 / gas[0]
    gas_velocity = [gas[1] * inv, gas[2] * inv, gas[3] * inv]
    gas_temp = pressure_of(gas) * inv
    vapour = gas[5] * inv
    mass, temp = drop[3], drop[4]
    root = jnp.sqrt(mass)
    inv_root = 1.0 / root
    new_mass = mass * jnp.exp(-TIME_STEP * EVAP_RATE * gas_temp * inv_root / (1.0 + vapour * vapour))
    drag = jnp.exp((-TIME_STEP / DRAG_RELAX_TIME) * inv_root)
    warm = jnp.exp((-TIME_STEP / HEATING_RELAX) * inv_root)
    new_velocity = [gas_velocity[d] + (drop[d] - gas_velocity[d]) * drag for d in range(3)]
    new_temp = gas_temp + (temp - gas_temp) * warm
    lost = mass - new_mass
    momentum = [mass * drop[d] - new_mass * new_velocity[d] for d in range(3)]
    before = drop[0] * drop[0] + drop[1] * drop[1] + drop[2] * drop[2]
    after = new_velocity[0] * new_velocity[0] + new_velocity[1] * new_velocity[1] + new_velocity[2] * new_velocity[2]
    energy = 0.5 * (mass * before - new_mass * after) + LIQUID_HEAT * (mass * temp - new_mass * new_temp)
    return new_velocity + [new_mass, new_temp], [lost] + momentum + [energy]


def row_sums(parts):
    count = len(parts)
    row_id = lax.broadcasted_iota(jnp.int32, parts[0].shape, 0)
    step = 1
    while step < count:
        low = (row_id // step) % 2 == 0
        parts = [
            jnp.where(low, a, b) + pltpu.roll(jnp.where(low, b, a), step, 0) for a, b in zip(parts[::2], parts[1::2])
        ]
        step *= 2
    return parts[0]


def split_three(v):
    head = v.astype(BF16)
    rest = v - head.astype(F32)
    middle = rest.astype(BF16)
    return head, middle, (rest - middle.astype(F32)).astype(BF16)


def kernel(
    sizes, counts_h, order_h, gas_h, parcels_h, cells_h,
    gas_out, moved,
    counts_v, order_v, gas, parcels, cells, fetch,
    faces, ghosts, states, change, stepped, table, hot, high_hot, sources, live, *rest,
):
    spreads, rest = rest[:QUARTERS], rest[QUARTERS:]
    choice, blocks, own_blocks, going, coming, arrived, count_out, count_in = rest[:8]
    face_send, face_recv, move_send, move_recv, count_send, count_recv = rest[8:]
    place = [lax.axis_index(a) for a in AXES]
    planes, rows, lanes = gas.shape[1:]
    slots = parcels.shape[1]
    cap = slots // 4
    group = 8
    chunks = slots // group
    half = planes // 2
    wide = half * rows

    inputs = ((gas_h, gas), (counts_h, counts_v), (order_h, order_v), (cells_h, cells), (parcels_h, parcels))
    fetches = [pltpu.make_async_copy(src, dst, fetch.at[i]) for i, (src, dst) in enumerate(inputs)]
    for copy in fetches:
        copy.start()

    def has(k, side):
        return place[k] > 0 if side == 0 else place[k] < sizes[k] - 1

    def neighbour(k, side):
        return {AXES[k]: lax.rem(place[k] + (sizes[k] - 1 if side == 0 else 1), sizes[k])}

    def copy_to(k, side, src, dst, send, recv):
        return pltpu.make_async_remote_copy(
            src_ref=src, dst_ref=dst, send_sem=send, recv_sem=recv,
            device_id=neighbour(k, side), device_id_type=MESH,
        )

    def face_copy(turn, k, side):
        return copy_to(
            k, side, faces.at[turn, k, side], ghosts.at[turn, k, 1 - side],
            face_send.at[turn, k, side], face_recv.at[turn, k, 1 - side],
        )

    def count_copy(side):
        return copy_to(0, side, count_out.at[side], count_in.at[1 - side], count_send.at[side], count_recv.at[1 - side])

    def move_copy(side):
        return copy_to(0, side, going.at[side], coming.at[1 - side], move_send.at[side], move_recv.at[1 - side])

    links = [(k, side) for k in range(3) for side in range(2) if sizes[k] > 1]

    barrier = pltpu.get_barrier_semaphore()
    arrivals = 0
    for k, side in links:
        @pl.when(has(k, side))
        def _():
            pl.semaphore_signal(barrier, inc=1, device_id=neighbour(k, side), device_id_type=MESH)
        arrivals = arrivals + has(k, side).astype(jnp.int32)

    for copy in fetches[:4]:
        copy.wait()
    kept, forward, backward = [counts_v[0:1, i : i + 1] for i in range(3)]
    pack_faces(gas, faces.at[0])
    count_out[0] = jnp.broadcast_to(backward, count_out.shape[1:])
    count_out[1] = jnp.broadcast_to(forward, count_out.shape[1:])
    for side in range(2):
        @pl.when(jnp.logical_not(has(0, side)))
        def _():
            count_in[side] = jnp.zeros(count_in.shape[1:], jnp.int32)
            coming[side] = jnp.zeros(coming.shape[1:], F32)

    pl.semaphore_wait(barrier, arrivals)

    def send_faces(turn):
        for k in range(3):
            for side in range(2):
                if (k, side) in links:
                    @pl.when(has(k, side))
                    def _():
                        face_copy(turn, k, side).start()

                @pl.when(jnp.logical_not(has(k, side)))
                def _():
                    ghosts[turn, k, side] = faces[turn, k, side]

    def receive_faces(turn):
        for k, side in links:
            @pl.when(has(k, side))
            def _():
                face_copy(turn, k, 1 - side).wait_recv()

    send_faces(0)
    for side in range(2):
        if sizes[0] > 1:
            @pl.when(has(0, side))
            def _():
                count_copy(side).start()

    def build(i, carry):
        cell = cells[pl.ds(i * group, group), :]
        column = ((cell % lanes) + (cell // (lanes * wide)) * lanes).astype(F32)
        high = ((cell // lanes) % wide).astype(F32)
        column_id = lax.broadcasted_iota(jnp.int32, (2 * lanes, lanes), 0).astype(F32).astype(BF16)
        row_id = lax.broadcasted_iota(jnp.int32, (wide, lanes), 0).astype(F32).astype(BF16)
        one, none = jnp.ones((), BF16), jnp.zeros((), BF16)
        for j in range(group):
            here = pl.ds(pl.multiple_of((i * group + j) * lanes, lanes), lanes)
            match = jnp.broadcast_to(column[j : j + 1, :], column_id.shape).astype(BF16) == column_id
            hot[:, here] = jnp.where(match, one, none)
            match = jnp.broadcast_to(high[j : j + 1, :], row_id.shape).astype(BF16) == row_id
            high_hot[:, here] = jnp.where(match, one, none)
        return carry

    inner_change(gas, change)
    edge_states(faces.at[0], states)
    lax.fori_loop(0, chunks // 2, build, 0)
    receive_faces(0)
    both = full_change(change, faces.at[0], states, ghosts.at[0])
    for c in range(6):
        stepped[c] = gas[c] + TIME_STEP * both[c]
    pack_faces(stepped, faces.at[1])
    send_faces(1)
    inner_change(stepped, change)
    edge_states(faces.at[1], states)

    lax.fori_loop(chunks // 2, chunks, build, 0)
    fetches[4].wait()
    slot_id = lax.broadcasted_iota(jnp.int32, (slots, slots), 0)
    turn_id = lax.broadcasted_iota(jnp.int32, (slots, slots), 1)
    used = (order_v[...] == slot_id) & (turn_id < kept + forward + backward)
    used = jnp.sum(jnp.where(used, 1.0, 0.0), axis=1, keepdims=True)
    live[...] = jnp.broadcast_to(used, live.shape)

    rows_out = slots + 2 * cap
    take_id = lax.broadcasted_iota(jnp.int32, (rows_out, slots), 0)
    from_id = lax.broadcasted_iota(jnp.int32, (rows_out, slots), 1)
    spot = jnp.where(take_id < slots, take_id, take_id - slots + kept)
    spot = jnp.where(take_id < slots + cap, spot, take_id - slots - cap + kept + forward)
    origin = jnp.where(from_id == spot, order_v[...].astype(F32), 0.0)
    origin = jnp.sum(origin, axis=1, keepdims=True)
    wide_id = lax.broadcasted_iota(jnp.int32, choice.shape, 1) % slots
    take_id = lax.broadcasted_iota(jnp.int32, choice.shape, 0)
    chosen = (wide_id.astype(F32) == origin) & ((take_id < kept) | (take_id >= slots))
    choice[...] = jnp.where(chosen, 1.0, 0.0).astype(BF16)

    receive_faces(1)
    both = full_change(change, faces.at[1], states, ghosts.at[1])
    for c in range(6):
        v = 0.5 * gas[c] + 0.5 * (stepped[c] + TIME_STEP * both[c])
        stepped[c] = v
        for part in range(2):
            terms = split_three(v[part * half : (part + 1) * half].reshape(wide, lanes))
            for t in range(2):
                start = (6 * t + c) * wide
                table[start : start + wide, part * lanes : (part + 1) * lanes] = terms[t]

    def spread_out(i, spread, n):
        source = [sources[i, c] for c in range(5)]
        head = [v.astype(BF16).astype(F32) for v in source]
        rest = [v - h for v, h in zip(source, head)]
        for j in range(group):
            match = high_hot[:, (i * group + j) * lanes : (i * group + j + 1) * lanes]
            here = slice((n * group + j) * lanes, (n * group + j + 1) * lanes)
            for c, v in enumerate(head + rest):
                term = jnp.broadcast_to(v[j : j + 1, :], (wide, lanes)).astype(BF16)
                spread[c * wide : (c + 1) * wide, here] = match * term

    def gather(i, carry):
        for n in range(2):
            gather_chunk(2 * i + n)
        return carry

    def gather_chunk(i):
        block = pl.ds(pl.multiple_of(i * group, group), group)
        cell = cells[block, :]
        high = (cell // lanes) % wide
        row_id = lax.broadcasted_iota(jnp.int32, (wide, lanes), 0)
        every = pl.ds(pl.multiple_of(i * group * lanes, group * lanes), group * lanes)
        found = jnp.dot(table[...], hot[:, every], preferred_element_type=F32)
        parts = [[None] * group for _ in range(6)]
        for j in range(group):
            here = slice(j * lanes, (j + 1) * lanes)
            match = row_id == high[j : j + 1, :]
            for c in range(6):
                v = found[c * wide : (c + 1) * wide, here] + found[(6 + c) * wide : (7 + c) * wide, here]
                v = jnp.where(match, v, 0.0)
                parts[c][j] = sum(v[r : r + group] for r in range(group, wide, group)) + v[:group]
        got = [row_sums(v) for v in parts]
        new, source = parcel_update([parcels[d, block, :] for d in range(5)], got)
        for d in range(5):
            for part, term in enumerate(split_three(new[d])):
                blocks[d, pl.ds(pl.multiple_of(part * slots + i * group, group), group), :] = term.astype(F32)
        for c in range(5):
            sources[i, c] = source[c] * live[block, :]

    lax.fori_loop(0, chunks // 2, gather, 0)

    for d in range(5):
        sorted_blocks = jnp.dot(choice[...], blocks[d].astype(BF16), preferred_element_type=F32)
        own_blocks[d] = sorted_blocks[:slots]
        going[1, d] = sorted_blocks[slots : slots + cap]
        going[0, d] = sorted_blocks[slots + cap :]
    for side in range(2):
        if sizes[0] > 1:
            @pl.when(has(0, side))
            def _():
                move_copy(side).start()

    share = chunks // len(spreads)
    total = 0.0
    for q, spread in enumerate(spreads):
        for n in range(share):
            spread_out(q * share + n, spread, n)
        there = slice(q * share * group * lanes, (q + 1) * share * group * lanes)
        total = total + lax.dot_general(
            spread[...], hot[:, there], (((1,), (1,)), ((), ())), preferred_element_type=F32
        )
    for c in range(6):
        s = 0 if c == 5 else c
        summed = total[s * wide : (s + 1) * wide, :] + total[(5 + s) * wide : (6 + s) * wide, :]
        for part in range(2):
            part_sum = summed[:, part * lanes : (part + 1) * lanes].reshape(half, rows, lanes)
            here = slice(part * half, (part + 1) * half)
            gas_out[c, here] = stepped[c, here] + part_sum

    for side in range(2):
        if sizes[0] > 1:
            @pl.when(has(0, side))
            def _():
                count_copy(1 - side).wait_recv()
                move_copy(1 - side).wait_recv()

    place_shape = (slots, 6 * cap)
    slot_id = lax.broadcasted_iota(jnp.int32, place_shape, 0)
    block_id = lax.broadcasted_iota(jnp.int32, place_shape, 1) % (2 * cap)
    lower = jnp.broadcast_to(count_in[0, 0:1, : 6 * cap], place_shape)
    upper = jnp.broadcast_to(count_in[1, 0:1, : 6 * cap], place_shape)
    from_lower = (slot_id - kept == block_id) & (block_id < cap) & (block_id < lower)
    above = block_id - cap
    from_upper = (slot_id - kept - lower == above) & (above >= 0) & (above < upper)
    fill = jnp.where(from_lower | from_upper, 1.0, 0.0).astype(BF16)
    for d in range(5):
        for side in range(2):
            for part, term in enumerate(split_three(coming[side, d])):
                start = part * 2 * cap + side * cap
                arrived[d, start : start + cap, :] = term
        moved[d] = own_blocks[d] + jnp.dot(fill, arrived[d], preferred_element_type=F32)

    for turn in range(2):
        for k, side in links:
            @pl.when(has(k, side))
            def _():
                face_copy(turn, k, side).wait_send()
    for side in range(2):
        if sizes[0] > 1:
            @pl.when(has(0, side))
            def _():
                count_copy(side).wait_send()
                move_copy(side).wait_send()


def body(sizes, gas, parcels, home_cell_index, order, counts):
    planes, rows, lanes = gas.shape[1:]
    parcels = jnp.transpose(parcels, (1, 0, 2))
    slots = parcels.shape[1]
    group = 8
    chunks = slots // group
    wide = planes // 2 * rows
    cap = slots // 4
    vmem = pl.BlockSpec(memory_space=pltpu.VMEM)
    hbm = pl.BlockSpec(memory_space=pltpu.HBM)
    dma = pltpu.SemaphoreType.DMA
    gas_out, moved = pl.pallas_call(
        functools.partial(kernel, sizes),
        out_shape=(pltpu.VMEM(gas.shape, F32), pltpu.VMEM(parcels.shape, F32)),
        in_specs=[hbm] * 5,
        out_specs=(vmem, vmem),
        scratch_shapes=[
            pltpu.VMEM(counts.shape, jnp.int32),
            pltpu.VMEM(order.shape, jnp.int32),
            pltpu.VMEM(gas.shape, F32),
            pltpu.VMEM(parcels.shape, F32),
            pltpu.VMEM(home_cell_index.shape, jnp.int32),
            dma((5,)),
            pltpu.VMEM((2, 3, 2, 6, rows, lanes), F32),
            pltpu.VMEM((2, 3, 2, 6, rows, lanes), F32),
            pltpu.VMEM((3, 2, 7, rows, lanes), F32),
            pltpu.VMEM(gas.shape, F32),
            pltpu.VMEM(gas.shape, F32),
            pltpu.VMEM((12 * wide, 2 * lanes), BF16),
            pltpu.VMEM((2 * lanes, slots * lanes), BF16),
            pltpu.VMEM((wide, slots * lanes), BF16),
            pltpu.VMEM((chunks, 5, group, lanes), F32),
            pltpu.VMEM((slots, lanes), F32),
            *[pltpu.VMEM((10 * wide, slots * lanes // QUARTERS), BF16)] * QUARTERS,
            pltpu.VMEM((slots + 2 * cap, 3 * slots), BF16),
            pltpu.VMEM((5, 3 * slots, lanes), F32),
            pltpu.VMEM(parcels.shape, F32),
            pltpu.VMEM((2, 5, cap, lanes), F32),
            pltpu.VMEM((2, 5, cap, lanes), F32),
            pltpu.VMEM((5, 6 * cap, lanes), BF16),
            pltpu.VMEM((2, 8, lanes), jnp.int32),
            pltpu.VMEM((2, 8, lanes), jnp.int32),
            dma((2, 3, 2)), dma((2, 3, 2)), dma((2,)), dma((2,)), dma((2,)), dma((2,)),
        ],
        compiler_params=pltpu.CompilerParams(
            collective_id=0, has_side_effects=True, vmem_limit_bytes=48 * 1024 * 1024
        ),
    )(*[pltpu.with_memory_space_constraint(v, pltpu.HBM) for v in (counts, order, gas, parcels, home_cell_index)])
    return gas_out, jnp.transpose(moved, (1, 0, 2))


def solution(mesh):
    in_specs = (
        P(None, "gx", "gy", "gz"),
        P(("gx", "gy", "gz"), None, None),
        P(("gx", "gy", "gz"), None),
        P(("gx", "gy", "gz"), None),
        P(("gx", "gy", "gz"), None),
    )
    out_specs = (P(None, "gx", "gy", "gz"), P(("gx", "gy", "gz"), None, None))
    sizes = tuple(mesh.shape[a] for a in AXES)
    return jax.shard_map(
        functools.partial(body, sizes), mesh=mesh, in_specs=in_specs, out_specs=out_specs, check_vma=False
    )
```
